512 devices in a mesh: ctx: 64 (over z, x_hi, core), kvh: 8 (over y, x_lo).
Axes of the slice: x: 4 (x_hi: 2, x_lo: 2; x = x_hi * 2 + x_lo), y: 4, z: 16, core: 2. Of those that a mesh axis runs over, the one named last changes fastest.
Arguments:
- query: bfloat16 [24576, 4096], P('ctx', 'kvh'), may hold values from -256 to 256
- keys_values: bfloat16 [24576, 2048], P('ctx', 'kvh'), may hold values from -4 to 4
- doc_start: int32 [24576], P('ctx'), may hold values from 0 to 24528, as said below
- scale_index: int32 [192], replicated, may hold values from 0 to 63
- scale_table: float32 [64, 16], P(None, 'kvh'), may hold values from 0.5 to 2
- out_weight: bfloat16 [4096, 4096], P('kvh'), may hold values from -0.09375 to 0.09375
Outputs:
- projected: bfloat16 [24576, 4096], P(('ctx', 'kvh'))
The draws below stay inside these ranges and needn't reach their ends.
Inputs may be any that keep to these rules, and one draw needn't show every extreme that they name: doc_start[i] is the first position of the document that holds token i; documents are consecutive runs of 48 to 6144 tokens, except that the document just before the last may be cut short; the last document is exactly the final 48 tokens, and one of the first three documents has exactly 6144 tokens.
All inputs are finite; a program needn't handle non-finite values.
Results may differ from the reference program's by a relative error of at most 0.019.
Values may be sent and summed in bfloat16 or wider, within the bound.
No kernel may reach another device: no remote copies, remote signals or barrier semaphores. Data moves between devices by JAX's collectives and lax.ppermute only.
A program may use at most 64 MiB of HBM per device.

```python
import math
import jax
import jax.numpy as jnp
from jax import lax

H = 32
KVH = 8
HD = 128
D = 4096
TOK_DEV = 384
SBLK = 128
SCALES = 64
REACH = 16
MAXDOC = 6144
MINDOC = 48
TOKENS = 24576
N_CTX = 64
N_KVH = 8


def key_fields(key):
    sub_keys = jax.random.split(key, 1)
    shape = (TOKENS, KVH, 2, HD)
    normal_part = jnp.clip(jax.random.normal(sub_keys[0], shape, jnp.float32), -3.5, 3.5)
    base = normal_part
    fields = base
    key_part = fields[:, :, 0, :]
    fields = jnp.stack([key_part, fields[:, :, 1, :]], axis=2)
    return fields


def draw_keys_values(key, part):
    fields = key_fields(key)
    return fields.reshape(TOKENS, 2 * KVH * HD).astype(jnp.bfloat16)


def draw_query(key, part):
    shape = (TOKENS, KVH, H // KVH, HD)
    own_key = jax.random.fold_in(key, 5)
    result = jnp.clip(jax.random.normal(own_key, shape, jnp.float32), -3.5, 3.5)
    return result.reshape(TOKENS, H * HD).astype(jnp.bfloat16)


def draw_doc_start(key, part):
    key = jax.random.fold_in(key, 17)
    length_key, pick_key = jax.random.split(key)
    doc_count = TOKENS // MINDOC + 2
    lengths = jax.random.randint(length_key, (doc_count,), MINDOC, MAXDOC + 1, dtype=jnp.int32)
    chosen = jax.random.randint(pick_key, (), 0, 3, dtype=jnp.int32)
    lengths = jnp.where(jnp.arange(doc_count, dtype=jnp.int32) == chosen, MAXDOC, lengths)
    doc_ends = jnp.cumsum(lengths).astype(jnp.int32)
    doc_starts = doc_ends - lengths
    position = jnp.arange(TOKENS, dtype=jnp.int32)
    owner_index = jnp.searchsorted(doc_ends, position, side='right')
    drawn = doc_starts[owner_index].astype(jnp.int32)
    last_begin = TOKENS - MINDOC
    return jnp.where(position >= last_begin, last_begin, drawn).astype(jnp.int32)


def with_ends(entries, rng, least, largest):
    longest = entries.shape.index(max(entries.shape))
    spots = []
    for shift in (0, 1):
        where = [jax.random.randint(jax.random.fold_in(rng, axis), (), 0, length) for axis, length in enumerate(entries.shape)]
        where[longest] = (where[longest] + shift) % entries.shape[longest]
        spots.append(tuple(where))
    return entries.at[spots[0]].set(least).at[spots[1]].set(largest)


def shard_levels(stream_key, extent, cuts, smallest, high):
    gain, own = 1.0, jax.random.fold_in(stream_key, 6)
    for dim, parts in cuts:
        heights = jnp.exp(jax.random.uniform(jax.random.fold_in(own, dim), (parts,), jnp.float32, smallest / len(cuts), high / len(cuts)))
        gain = gain * jnp.repeat(heights, extent[dim] // parts).reshape([-1 if axis == dim else 1 for axis in range(len(extent))])
    return gain


def normal_values(key, extent, scale, reach, pieces=(), kind=jnp.bfloat16):
    loudness = shard_levels(key, extent, pieces, -0.22, 0.18) if pieces else 1.0
    values = jax.random.normal(key, extent, jnp.float32) * scale * loudness
    return jnp.minimum(jnp.maximum(values, -reach), reach).astype(kind)


def setup_inputs(seed: int = 0) -> dict:
    streams_of = jax.random.split(jax.random.key(seed), 7)
    query = draw_query(jax.random.fold_in(streams_of[6], 71), 0)
    keys_values = draw_keys_values(jax.random.fold_in(streams_of[6], 71), 0)
    doc_start = draw_doc_start(jax.random.fold_in(streams_of[6], 71), 0)
    scale_index = with_ends(jax.random.randint(streams_of[3], (TOKENS // SBLK,), 0, SCALES), jax.random.fold_in(streams_of[3], 1), 0, SCALES - 1).astype(jnp.int32)
    scale_table = jnp.clip(jnp.exp(math.log(2.0) - 1.3862944 * jax.random.uniform(streams_of[4], (SCALES, 2 * KVH), jnp.float32) ** shard_levels(streams_of[4], (SCALES, 2 * KVH), ((1, 8),), -0.2, 0.2)), 0.5, 2.0)
    out_weight = normal_values(streams_of[5], (H * HD, D), (H * HD) ** -0.5, 0.09375, ((0, 8),))
    return dict(query=query, keys_values=keys_values, doc_start=doc_start, scale_index=scale_index, scale_table=scale_table, out_weight=out_weight)


def reference(query, keys_values, doc_start, scale_index, scale_table, out_weight):
    q_groups = H // KVH
    per_block = scale_table[scale_index]
    per_key = jnp.repeat(per_block, SBLK, axis=0)
    key_scale = per_key[:, 0::2]
    value_scale = per_key[:, 1::2]
    window = (REACH + 1) * TOK_DEV
    lead_rows = REACH * TOK_DEV
    kv_padded = jnp.concatenate([jnp.zeros((lead_rows, 2 * KVH * HD), keys_values.dtype), keys_values], 0)
    ks_padded = jnp.concatenate([jnp.ones((lead_rows, KVH), key_scale.dtype), key_scale], 0)
    vs_padded = jnp.concatenate([jnp.ones((lead_rows, KVH), value_scale.dtype), value_scale], 0)
    query_heads = query.reshape(TOKENS, KVH, q_groups, HD)
    score_factor = 1.0 / math.sqrt(HD)

    def one_block(block_index):
        begin = (block_index * TOK_DEV).astype(jnp.int32)
        q_block = lax.dynamic_slice_in_dim(query_heads, begin, TOK_DEV, 0).astype(jnp.float32)
        kv_window = lax.dynamic_slice_in_dim(kv_padded, begin, window, 0).reshape(window, KVH, 2, HD).astype(jnp.float32)
        ks_window = lax.dynamic_slice_in_dim(ks_padded, begin, window, 0)
        vs_window = lax.dynamic_slice_in_dim(vs_padded, begin, window, 0)
        key_pos = begin - lead_rows + jnp.arange(window, dtype=jnp.int32)
        query_pos = begin + jnp.arange(TOK_DEV, dtype=jnp.int32)
        doc_first = lax.dynamic_slice_in_dim(doc_start, begin, TOK_DEV, 0)
        visible = (key_pos[None, :] >= doc_first[:, None]) & (key_pos[None, :] <= query_pos[:, None])
        scores = jnp.einsum('tkgd,skd->ktgs', q_block, kv_window[:, :, 0, :])
        scores = scores * (ks_window.T * score_factor)[:, None, None, :]
        scores = jnp.where(visible[None, :, None, :], scores, -jnp.inf)
        row_max = lax.optimization_barrier(jnp.max(scores, axis=3, keepdims=True))
        probs = jnp.exp(scores - row_max)
        row_total = lax.optimization_barrier(jnp.sum(probs, axis=3))
        weights = lax.optimization_barrier((probs * vs_window.T[:, None, None, :]).astype(jnp.bfloat16)).astype(jnp.float32)
        mixed = jnp.einsum('ktgs,skd->ktgd', weights, kv_window[:, :, 1, :]) / row_total[..., None]
        return jnp.transpose(mixed, (1, 0, 2, 3)).reshape(TOK_DEV, H * HD).astype(jnp.bfloat16)
    attn = lax.map(one_block, jnp.arange(N_CTX, dtype=jnp.int32)).reshape(TOKENS, H * HD)
    group_cols = H * HD // N_KVH
    summed = jnp.zeros((TOKENS, D), jnp.float32)
    for group_index in range(N_KVH):
        low = group_index * group_cols
        partial_value = jnp.dot(attn[:, low:low + group_cols], out_weight[low:low + group_cols], preferred_element_type=jnp.float32)
        summed = summed + lax.optimization_barrier(partial_value.astype(jnp.bfloat16)).astype(jnp.float32)
    return summed.astype(jnp.bfloat16)
```

```python
import functools
import math

import jax
import jax.numpy as jnp
from jax import lax
from jax.experimental import pallas as pl
from jax.experimental.pallas import tpu as pltpu
from jax.sharding import PartitionSpec as P

H = 32
KVH = 8
HD = 128
SBLK = 128
SCALES = 64
GROUPS = H // KVH
PLANE = 4
NEG = -1e30
FACTOR = math.log2(math.e) / math.sqrt(HD)


def attend_kernel(
    counts, first, final, my_ref, src_ref, index_ref, table_ref, doc_ref, starts_ref, query_ref, *rest
):
    pieces, rest = rest[: len(counts)], rest[len(counts) :]
    if not first:
        (acc_in, max_in), rest = rest[:2], rest[2:]
    if final:
        out_ref, rest = rest[0], rest[1:]
    acc_ref, max_ref, bias_ref, held, sems = rest
    tok = query_ref.shape[0]
    blocks = sum(counts)
    copies = []
    at = 0
    for i, count in enumerate(counts):
        copies.append(pltpu.make_async_copy(pieces[i], held.at[pl.ds(at * tok, count * tok)], sems.at[i]))
        copies[-1].start()
        at += count
    my = my_ref[0]
    low, high = doc_ref[0], doc_ref[tok - 1]
    if first:
        acc_ref[...] = jnp.zeros_like(acc_ref)
        max_ref[...] = jnp.full(max_ref.shape, NEG, jnp.float32)
    else:
        acc_ref[...] = acc_in[...]
        max_ref[...] = max_in[...]
    for copy in copies:
        copy.wait()

    def attend_block(step, masked):
        src = src_ref[step]
        base = src * (tok // SBLK)
        key_scales, value_scales = [], []
        for t in range(tok // SBLK):
            row = index_ref[base + t]
            key_scales.append(jnp.full((1, SBLK), table_ref[2 * row] * FACTOR, jnp.float32))
            value_scales.append(jnp.full((SBLK, HD), table_ref[2 * row + 1], jnp.float32))
        scale = jnp.concatenate(key_scales, 1)
        kv_rows = pl.ds(pl.multiple_of(step * tok, tok), tok)
        keys = held[kv_rows, :HD]
        values = held[kv_rows, HD:].astype(jnp.float32) * jnp.concatenate(value_scales, 0)
        values = jnp.concatenate([values.astype(jnp.bfloat16), jnp.ones((tok, HD), jnp.bfloat16)], 1)
        if masked:
            key_pos = src * tok + lax.broadcasted_iota(jnp.int32, (tok, tok), 1)
            query_pos = my * tok + lax.broadcasted_iota(jnp.int32, (tok, tok), 0)
            starts = jnp.concatenate([starts_ref[...]] * (tok // HD), 1)
            bias_ref[...] = jnp.where((key_pos >= starts) & (key_pos <= query_pos), 0.0, NEG)
        for h in range(GROUPS):
            rows = pl.ds(h * tok, tok)
            scores = lax.dot_general(
                query_ref[:, h * HD : (h + 1) * HD],
                keys,
                (((1,), (1,)), ((), ())),
                preferred_element_type=jnp.float32,
            )
            scores = scores * scale
            if masked:
                scores = scores + bias_ref[...]
            old_max = max_ref[rows, :]
            new_max = jnp.maximum(old_max, jnp.max(scores, axis=1, keepdims=True))
            carry = jnp.exp2(old_max - new_max)
            max_ref[rows, :] = new_max
            probs = jnp.exp2(scores - jnp.concatenate([new_max] * (tok // HD), 1)).astype(jnp.bfloat16)
            mixed = jnp.dot(probs, values, preferred_element_type=jnp.float32)
            acc_ref[rows, :] = acc_ref[rows, :] * jnp.concatenate([carry, carry], 1) + mixed

    def one_step(step, _):
        src = src_ref[step]
        visible = (src >= 0) & (src * tok + tok - 1 >= low) & (src <= my)
        partial = (src == my) | (src * tok < high)

        @pl.when(visible & partial)
        def _():
            attend_block(step, True)

        @pl.when(visible & jnp.logical_not(partial))
        def _():
            attend_block(step, False)

        return 0

    lax.fori_loop(0, blocks, one_step, 0)
    if final:
        for h in range(GROUPS):
            acc = acc_ref[pl.ds(h * tok, tok), :]
            out_ref[:, h * HD : (h + 1) * HD] = (acc[:, :HD] / acc[:, HD:]).astype(jnp.bfloat16)


def attend(my, src, common, pieces, state=None, final=False):
    query = common[-1]
    tok = query.shape[0]
    counts = tuple(piece.shape[0] // tok for piece in pieces)
    vmem, smem = pl.BlockSpec(memory_space=pltpu.VMEM), pl.BlockSpec(memory_space=pltpu.SMEM)
    state_shape = (
        jax.ShapeDtypeStruct((GROUPS * tok, 2 * HD), jnp.float32),
        jax.ShapeDtypeStruct((GROUPS * tok, HD), jnp.float32),
    )
    scratch = [
        pltpu.VMEM((tok, tok), jnp.float32),
        pltpu.VMEM((sum(counts) * tok, 2 * HD), jnp.bfloat16),
        pltpu.SemaphoreType.DMA((len(counts),)),
    ]
    if final:
        out_shape, out_specs = jax.ShapeDtypeStruct((tok, GROUPS * HD), jnp.bfloat16), vmem
        scratch = [pltpu.VMEM(s.shape, s.dtype) for s in state_shape] + scratch
    else:
        out_shape, out_specs = state_shape, (vmem, vmem)
    flops = sum(counts) * GROUPS * tok * tok * HD * 4
    return pl.pallas_call(
        functools.partial(attend_kernel, counts, state is None, final),
        out_shape=out_shape,
        in_specs=[smem] * 5
        + [vmem] * 2
        + [pl.BlockSpec(memory_space=pl.ANY)] * len(pieces)
        + [vmem] * (0 if state is None else 2),
        out_specs=out_specs,
        scratch_shapes=scratch,
        compiler_params=pltpu.CompilerParams(vmem_limit_bytes=40 << 20),
        cost_estimate=pl.CostEstimate(flops=3 * flops, bytes_accessed=4 << 20, transcendentals=0),
    )(my, src, *common, *pieces, *(state or ()))


def local(query, keys_values, doc_start, scale_index, scale_table, out_weight):
    tok = query.shape[0]
    ctx_count = lax.axis_size("ctx")
    my = lax.axis_index("ctx").astype(jnp.int32)
    plane = my // PLANE
    groups = [[PLANE * i + j for j in range(PLANE)] for i in range(ctx_count // PLANE)]
    starts = jnp.broadcast_to(doc_start[:, None], (tok, HD))
    common = (scale_index, scale_table.reshape(-1), doc_start, starts, query)

    def forward(block):
        return lax.ppermute(block, "ctx", [(i, i + PLANE) for i in range(ctx_count - PLANE)])

    def gathered(block):
        return lax.all_gather(block, "ctx", axis_index_groups=groups, tiled=True)

    def sources(*back):
        src = jnp.concatenate([(plane - k) * PLANE + jnp.arange(PLANE, dtype=jnp.int32) for k in back])
        return jnp.where(src == my, -1, src)

    moving = keys_values
    planes = [gathered(moving)]
    for _ in range(PLANE):
        moving = forward(moving)
        planes.append(gathered(moving))
    state = attend(my[None], my[None], common, [keys_values])
    state = attend(my[None], sources(0, 1), common, planes[0:2], state)
    state = attend(my[None], sources(2, 3), common, planes[2:4], state)
    attn = attend(my[None], sources(4), common, planes[4:5], state, True)
    shares = lax.axis_size("kvh")
    partial = jnp.dot(attn, out_weight, preferred_element_type=jnp.float32).astype(jnp.bfloat16)
    pieces = lax.all_to_all(partial.reshape(shares, tok // shares, -1), "kvh", 0, 0)
    return jnp.sum(pieces.astype(jnp.float32), axis=0).astype(jnp.bfloat16)


def solution(mesh):
    placed = (P("ctx", "kvh"), P("ctx", "kvh"), P("ctx"), P(), P(None, "kvh"), P("kvh", None))
    return jax.shard_map(
        local, mesh=mesh, in_specs=placed, out_specs=P(("ctx", "kvh"), None), check_vma=False
    )
```

```python
import functools
import math

import jax
import jax.numpy as jnp
from jax import lax
from jax.experimental import pallas as pl
from jax.experimental.pallas import tpu as pltpu
from jax.sharding import PartitionSpec as P

H = 32
KVH = 8
HD = 128
SBLK = 128
SCALES = 64
GROUPS = H // KVH
PLANE = 4
NEG = -1e30
FACTOR = math.log2(math.e) / math.sqrt(HD)


def attend_kernel(
    counts, groups, first, final, index_ref, table_ref, starts_ref, query_ref, *rest
):
    pieces, rest = rest[: len(counts)], rest[len(counts) :]
    if not first:
        (acc_in, max_in), rest = rest[:2], rest[2:]
    if final:
        out_ref, rest = rest[0], rest[1:]
    acc_ref, max_ref, bias_ref, held, sems = rest
    tok = query_ref.shape[0]
    copies = []
    at = 0
    for i, count in enumerate(counts):
        copies.append(pltpu.make_async_copy(pieces[i], held.at[pl.ds(at * tok, count * tok)], sems.at[i]))
        copies[-1].start()
        at += count
    low, high, my = [index_ref[index_ref.shape[0] - 3 + i] for i in range(3)]
    if first:
        acc_ref[...] = jnp.zeros_like(acc_ref)
        max_ref[...] = jnp.full(max_ref.shape, NEG, jnp.float32)
    else:
        acc_ref[...] = acc_in[...]
        max_ref[...] = max_in[...]
    for copy in copies:
        copy.wait()

    def attend_blocks(step, src, count, masked):
        key_scales, value_scales = [], []
        for t in range(count * tok // SBLK):
            row = index_ref[(src - 2 * (t // (tok // SBLK))) * (tok // SBLK) + t % (tok // SBLK)]
            key_scales.append(jnp.full((1, SBLK), table_ref[2 * row] * FACTOR, jnp.float32))
            value_scales.append(jnp.full((SBLK, HD), table_ref[2 * row + 1], jnp.float32))
        scale = jnp.concatenate(key_scales, 1)
        width = count * tok
        kv_rows = pl.ds(pl.multiple_of(step * tok, tok), width)
        keys = held[kv_rows, :HD]
        values = held[kv_rows, HD:].astype(jnp.float32) * jnp.concatenate(value_scales, 0)
        values = jnp.concatenate([values.astype(jnp.bfloat16), jnp.ones((width, HD), jnp.bfloat16)], 1)
        if masked:
            key_pos = src * tok + lax.broadcasted_iota(jnp.int32, (tok, tok), 1)
            query_pos = my * tok + lax.broadcasted_iota(jnp.int32, (tok, tok), 0)
            starts = jnp.concatenate([starts_ref[...]] * (tok // HD), 1)
            bias_ref[...] = jnp.where((key_pos >= starts) & (key_pos <= query_pos), 0.0, NEG)
        for h in range(GROUPS):
            rows = pl.ds(h * tok, tok)
            scores = lax.dot_general(
                query_ref[:, h * HD : (h + 1) * HD],
                keys,
                (((1,), (1,)), ((), ())),
                preferred_element_type=jnp.float32,
            )
            scores = scores * scale
            if masked:
                scores = scores + bias_ref[...]
            old_max = max_ref[rows, :]
            new_max = jnp.maximum(old_max, jnp.max(scores, axis=1, keepdims=True))
            carry = jnp.exp2(old_max - new_max)
            max_ref[rows, :] = new_max
            probs = jnp.exp2(scores - jnp.concatenate([new_max] * (width // HD), 1)).astype(jnp.bfloat16)
            mixed = jnp.dot(probs, values, preferred_element_type=jnp.float32)
            acc_ref[rows, :] = acc_ref[rows, :] * jnp.concatenate([carry, carry], 1) + mixed

    def one_block(step, src):
        @pl.when((src >= 0) & (src * tok + tok - 1 >= low) & (src <= my))
        def _():
            attend_blocks(step, src, 1, True)

    at = 0
    for count, mine, back in groups:
        newest = (my if mine else my ^ 1) - back
        if count == 1:
            one_block(at, newest)
        else:
            oldest = newest - 2 * (count - 1)
            whole = (oldest >= 0) & (oldest * tok >= high) & (newest < my)

            @pl.when(whole)
            def _(at=at, newest=newest, count=count):
                attend_blocks(at, newest, count, False)

            @pl.when(jnp.logical_not(whole))
            def _(at=at, newest=newest, count=count):
                def one_step(step, _):
                    one_block(at + step, newest - 2 * step)
                    return 0

                lax.fori_loop(0, count, one_step, 0)

        at += count
    if final:
        for h in range(GROUPS):
            acc = acc_ref[pl.ds(h * tok, tok), :]
            out_ref[:, h * HD : (h + 1) * HD] = (acc[:, :HD] / acc[:, HD:]).astype(jnp.bfloat16)


def attend(common, pieces, groups, state=None, final=False):
    query = common[-1]
    tok = query.shape[0]
    counts = tuple(piece.shape[0] // tok for piece in pieces)
    vmem, smem = pl.BlockSpec(memory_space=pltpu.VMEM), pl.BlockSpec(memory_space=pltpu.SMEM)
    state_shape = (
        jax.ShapeDtypeStruct((GROUPS * tok, 2 * HD), jnp.float32),
        jax.ShapeDtypeStruct((GROUPS * tok, HD), jnp.float32),
    )
    scratch = [
        pltpu.VMEM((tok, tok), jnp.float32),
        pltpu.VMEM((sum(counts) * tok, 2 * HD), jnp.bfloat16),
        pltpu.SemaphoreType.DMA((len(counts),)),
    ]
    if final:
        out_shape, out_specs = jax.ShapeDtypeStruct((tok, GROUPS * HD), jnp.bfloat16), vmem
        scratch = [pltpu.VMEM(s.shape, s.dtype) for s in state_shape] + scratch
    else:
        out_shape, out_specs = state_shape, (vmem, vmem)
    flops = sum(counts) * GROUPS * tok * tok * HD * 4
    return pl.pallas_call(
        functools.partial(attend_kernel, counts, groups, state is None, final),
        out_shape=out_shape,
        in_specs=[smem] * 2
        + [vmem] * 2
        + [pl.BlockSpec(memory_space=pl.ANY)] * len(pieces)
        + [vmem] * (0 if state is None else 2),
        out_specs=out_specs,
        scratch_shapes=scratch,
        compiler_params=pltpu.CompilerParams(vmem_limit_bytes=40 << 20),
        cost_estimate=pl.CostEstimate(flops=10 * flops, bytes_accessed=4 << 20, transcendentals=0),
    )(*common, *pieces, *(state or ()))


def local(query, keys_values, doc_start, scale_index, scale_table, out_weight):
    tok = query.shape[0]
    ctx_count = lax.axis_size("ctx")
    my = lax.axis_index("ctx").astype(jnp.int32)
    starts = jnp.broadcast_to(doc_start[:, None], (tok, HD))
    places = jnp.concatenate([scale_index, doc_start[:1], doc_start[-1:], my[None]])
    common = (places, scale_table.reshape(-1), starts, query)

    def shifted(block, distance):
        return lax.ppermute(block, "ctx", [(i, i + distance) for i in range(ctx_count - distance)])

    def swapped(*blocks):
        return lax.ppermute(jnp.concatenate(blocks), "ctx", [(i, i ^ 1) for i in range(ctx_count)])

    def after(block, *others):
        return lax.optimization_barrier((block, *others))[0]

    even, odd = [keys_values], []
    odd.append(shifted(even[0], 2))
    even.append(shifted(even[0], 4))
    state = attend(common, [even[0]], ((1, True, 0),))
    odd.append(shifted(even[1], 2))
    even.append(shifted(even[1], 4))
    state = attend(common, [odd[0], even[1]], ((2, True, 2),), state)
    odd.append(shifted(even[2], 2))
    even.append(shifted(even[2], 4))
    first_swap = swapped(even[0], odd[0], even[1], after(odd[1], even[2]))
    state = attend(common, [odd[1], even[2]], ((2, True, 6),), state)
    odd.append(shifted(even[3], 2))
    even.append(shifted(even[3], 4))
    groups = ((1, False, 0), (3, False, 2), (2, True, 10))
    state = attend(common, [first_swap, odd[2], even[3]], groups, state)
    second_swap = swapped(even[2], odd[2], even[3], after(odd[3], *state), even[4])
    state = attend(common, [odd[3], even[4]], ((2, True, 14),), state)
    attn = attend(common, [second_swap], ((4, False, 8), (1, False, 16)), state, True)
    shares = lax.axis_size("kvh")
    partial = jnp.dot(attn, out_weight, preferred_element_type=jnp.float32).astype(jnp.bfloat16)
    pieces = lax.all_to_all(partial.reshape(shares, tok // shares, -1), "kvh", 0, 0)
    return jnp.sum(pieces.astype(jnp.float32), axis=0).astype(jnp.bfloat16)


def solution(mesh):
    placed = (P("ctx", "kvh"), P("ctx", "kvh"), P("ctx"), P(), P(None, "kvh"), P("kvh", None))
    return jax.shard_map(
        local, mesh=mesh, in_specs=placed, out_specs=P(("ctx", "kvh"), None), check_vma=False
    )
```

```python
import functools
import math

import jax
import jax.numpy as jnp
from jax import lax
from jax.experimental import pallas as pl
from jax.experimental.pallas import tpu as pltpu
from jax.sharding import PartitionSpec as P

H = 32
KVH = 8
HD = 128
SBLK = 128
SCALES = 64
GROUPS = H // KVH
PLANE = 4
NEG = -1e30
FACTOR = math.log2(math.e) / math.sqrt(HD)


def attend_kernel(
    counts, groups, first, final, my_ref, doc_ref, index_ref, table_ref, starts_ref, query_ref, *rest
):
    pieces, rest = rest[: len(counts)], rest[len(counts) :]
    if not first:
        (acc_in, max_in), rest = rest[:2], rest[2:]
    if final:
        out_ref, rest = rest[0], rest[1:]
    acc_ref, max_ref, bias_ref, held, sems = rest
    tok = query_ref.shape[0]
    copies = []
    at = 0
    for i, count in enumerate(counts):
        copies.append(pltpu.make_async_copy(pieces[i], held.at[pl.ds(at * tok, count * tok)], sems.at[i]))
        copies[-1].start()
        at += count
    my, low, high = my_ref[0], doc_ref[0], doc_ref[tok - 1]
    if first:
        acc_ref[...] = jnp.zeros_like(acc_ref)
        max_ref[...] = jnp.full(max_ref.shape, NEG, jnp.float32)
    else:
        acc_ref[...] = acc_in[...]
        max_ref[...] = max_in[...]
    for copy in copies:
        copy.wait()

    def attend_blocks(step, src, count, masked):
        key_scales, value_scales = [], []
        for t in range(count * tok // SBLK):
            row = index_ref[(src - 4 * (t // (tok // SBLK))) * (tok // SBLK) + t % (tok // SBLK)]
            key_scales.append(jnp.full((1, SBLK), table_ref[row, 0] * FACTOR, jnp.float32))
            value_scales.append(jnp.full((SBLK, HD), table_ref[row, 1], jnp.float32))
        scale = jnp.concatenate(key_scales, 1)
        width = count * tok
        kv_rows = pl.ds(pl.multiple_of(step * tok, tok), width)
        keys = held[kv_rows, :HD]
        values = held[kv_rows, HD:].astype(jnp.float32) * jnp.concatenate(value_scales, 0)
        values = jnp.concatenate([values.astype(jnp.bfloat16), jnp.ones((width, HD), jnp.bfloat16)], 1)
        if masked:
            key_pos = src * tok + lax.broadcasted_iota(jnp.int32, (tok, tok), 1)
            query_pos = my * tok + lax.broadcasted_iota(jnp.int32, (tok, tok), 0)
            starts = jnp.concatenate([starts_ref[...]] * (tok // HD), 1)
            bias_ref[...] = jnp.where((key_pos >= starts) & (key_pos <= query_pos), 0.0, NEG)
        for h in range(GROUPS):
            rows = pl.ds(h * tok, tok)
            scores = lax.dot_general(
                query_ref[:, h * HD : (h + 1) * HD],
                keys,
                (((1,), (1,)), ((), ())),
                preferred_element_type=jnp.float32,
            )
            scores = scores * scale
            if masked:
                scores = scores + bias_ref[...]
            old_max = max_ref[rows, :]
            new_max = jnp.maximum(old_max, jnp.max(scores, axis=1, keepdims=True))
            carry = jnp.exp2(old_max - new_max)
            max_ref[rows, :] = new_max
            probs = jnp.exp2(scores - jnp.concatenate([new_max] * (width // HD), 1)).astype(jnp.bfloat16)
            mixed = jnp.dot(probs, values, preferred_element_type=jnp.float32)
            acc_ref[rows, :] = acc_ref[rows, :] * jnp.concatenate([carry, carry], 1) + mixed

    def one_block(step, src):
        @pl.when((src >= 0) & (src * tok + tok - 1 >= low) & (src <= my))
        def _():
            attend_blocks(step, src, 1, True)

    at = 0
    for count, mine, back in groups:
        newest = (my if mine else my ^ 1) - 2 * back
        if count == 1:
            one_block(at, newest)
        else:
            oldest = newest - 4 * (count - 1)
            whole = (oldest >= 0) & (oldest * tok >= high) & (newest < my)

            @pl.when(whole)
            def _(at=at, newest=newest, count=count):
                attend_blocks(at, newest, count, False)

            @pl.when(jnp.logical_not(whole))
            def _(at=at, newest=newest, count=count):
                def one_step(step, _):
                    one_block(at + step, newest - 4 * step)
                    return 0

                lax.fori_loop(0, count, one_step, 0)

        at += count
    if final:
        for h in range(GROUPS):
            acc = acc_ref[pl.ds(h * tok, tok), :]
            out_ref[:, h * HD : (h + 1) * HD] = (acc[:, :HD] / acc[:, HD:]).astype(jnp.bfloat16)


def attend(common, pieces, groups, state=None, final=False):
    query = common[-1]
    tok = query.shape[0]
    counts = tuple(piece.shape[0] // tok for piece in pieces)
    vmem, smem = pl.BlockSpec(memory_space=pltpu.VMEM), pl.BlockSpec(memory_space=pltpu.SMEM)
    state_shape = (
        jax.ShapeDtypeStruct((GROUPS * tok, 2 * HD), jnp.float32),
        jax.ShapeDtypeStruct((GROUPS * tok, HD), jnp.float32),
    )
    scratch = [
        pltpu.VMEM((tok, tok), jnp.float32),
        pltpu.VMEM((sum(counts) * tok, 2 * HD), jnp.bfloat16),
        pltpu.SemaphoreType.DMA((len(counts),)),
    ]
    if final:
        out_shape, out_specs = jax.ShapeDtypeStruct((tok, GROUPS * HD), jnp.bfloat16), vmem
        scratch = [pltpu.VMEM(s.shape, s.dtype) for s in state_shape] + scratch
    else:
        out_shape, out_specs = state_shape, (vmem, vmem)
    flops = sum(counts) * GROUPS * tok * tok * HD * 4
    return pl.pallas_call(
        functools.partial(attend_kernel, counts, groups, state is None, final),
        out_shape=out_shape,
        in_specs=[smem] * 4
        + [vmem] * 2
        + [pl.BlockSpec(memory_space=pl.ANY)] * len(pieces)
        + [vmem] * (0 if state is None else 2),
        out_specs=out_specs,
        scratch_shapes=scratch,
        compiler_params=pltpu.CompilerParams(vmem_limit_bytes=40 << 20),
        cost_estimate=pl.CostEstimate(flops=10 * flops, bytes_accessed=4 << 20, transcendentals=0),
    )(*common, *pieces, *(state or ()))


def local(query, keys_values, doc_start, scale_index, scale_table, out_weight):
    tok = query.shape[0]
    ctx_count = lax.axis_size("ctx")
    my = lax.axis_index("ctx").astype(jnp.int32)
    starts = jnp.broadcast_to(doc_start[:, None], (tok, HD))
    common = (my[None], doc_start, scale_index, scale_table, starts, query)

    def shifted(block, distance):
        return lax.ppermute(block, "ctx", [(i, i + distance) for i in range(ctx_count - distance)])

    def swapped(block):
        return lax.ppermute(block, "ctx", [(i, i ^ 1) for i in range(ctx_count)])

    def after(block, *others):
        return lax.optimization_barrier((block, *others))[0]

    from_2 = shifted(keys_values, 4)
    from_02 = jnp.concatenate([keys_values, from_2])
    from_46 = shifted(from_02, 8)
    from_13 = shifted(from_02, 2)
    from_57 = shifted(from_46, 2)
    from_8 = shifted(from_46[tok:], 4)
    other_1302 = swapped(jnp.concatenate([from_13, from_02]))
    state = attend(common, [keys_values, from_2], ((1, True, 0), (1, True, 2)))
    state = attend(common, [from_13], ((2, True, 1),), state)
    other_46 = swapped(after(from_46, *state))
    groups = ((2, True, 4), (2, False, 1), (1, False, 0), (1, False, 2), (2, False, 4))
    state = attend(common, [from_46, other_1302, other_46], groups, state)
    other_578 = swapped(jnp.concatenate([after(from_57, *state), from_8]))
    state = attend(common, [from_57, from_8], ((2, True, 5), (1, True, 8)), state)
    attn = attend(common, [other_578], ((2, False, 5), (1, False, 8)), state, True)
    shares = lax.axis_size("kvh")
    partial = jnp.dot(attn, out_weight, preferred_element_type=jnp.float32).astype(jnp.bfloat16)
    pieces = lax.all_to_all(partial.reshape(shares, tok // shares, -1), "kvh", 0, 0)
    return jnp.sum(pieces.astype(jnp.float32), axis=0).astype(jnp.bfloat16)


def solution(mesh):
    placed = (P("ctx", "kvh"), P("ctx", "kvh"), P("ctx"), P(), P(None, "kvh"), P("kvh", None))
    return jax.shard_map(
        local, mesh=mesh, in_specs=placed, out_specs=P(("ctx", "kvh"), None), check_vma=False
    )
```

```python
import functools
import math

import jax
import jax.numpy as jnp
from jax import lax
from jax.experimental import pallas as pl
from jax.experimental.pallas import tpu as pltpu
from jax.sharding import PartitionSpec as P

H = 32
KVH = 8
HD = 128
SBLK = 128
SCALES = 64
GROUPS = H // KVH
PLANE = 4
NEG = -1e30
FACTOR = math.log2(math.e) / math.sqrt(HD)


def attend_kernel(
    counts, groups, first, final, my_ref, doc_ref, index_ref, table_ref, starts_ref, query_ref, *rest
):
    pieces, rest = rest[: len(counts)], rest[len(counts) :]
    if not first:
        rest = rest[2:]
    acc_ref, max_ref, *rest = rest
    if final:
        out_ref, *rest = rest
    bias_ref, held, sems = rest
    tok = query_ref.shape[0]
    copies = []
    at = 0
    for i, count in enumerate(counts):
        copies.append(pltpu.make_async_copy(pieces[i], held.at[pl.ds(at * tok, count * tok)], sems.at[i]))
        copies[-1].start()
        at += count
    my, low, high = my_ref[0], doc_ref[0], doc_ref[tok - 1]
    if first:
        acc_ref[...] = jnp.zeros_like(acc_ref)
        max_ref[...] = jnp.full(max_ref.shape, NEG, jnp.float32)
    for copy in copies:
        copy.wait()

    def attend_blocks(step, src, count, masked):
        key_scales, value_scales = [], []
        for t in range(count * tok // SBLK):
            row = index_ref[(src - 4 * (t // (tok // SBLK))) * (tok // SBLK) + t % (tok // SBLK)]
            key_scales.append(jnp.full((1, SBLK), table_ref[row, 0] * FACTOR, jnp.float32))
            value_scales.append(jnp.full((SBLK, HD), table_ref[row, 1], jnp.float32))
        scale = jnp.concatenate(key_scales, 1)
        width = count * tok
        kv_rows = pl.ds(pl.multiple_of(step * tok, tok), width)
        keys = held[kv_rows, :HD]
        values = held[kv_rows, HD:].astype(jnp.float32) * jnp.concatenate(value_scales, 0)
        values = jnp.concatenate([values.astype(jnp.bfloat16), jnp.ones((width, HD), jnp.bfloat16)], 1)
        if masked:
            key_pos = src * tok + lax.broadcasted_iota(jnp.int32, (tok, tok), 1)
            query_pos = my * tok + lax.broadcasted_iota(jnp.int32, (tok, tok), 0)
            starts = jnp.concatenate([starts_ref[...]] * (tok // HD), 1)
            bias_ref[...] = jnp.where((key_pos >= starts) & (key_pos <= query_pos), 0.0, NEG)
        for h in range(GROUPS):
            rows = pl.ds(h * tok, tok)
            scores = lax.dot_general(
                query_ref[:, h * HD : (h + 1) * HD],
                keys,
                (((1,), (1,)), ((), ())),
                preferred_element_type=jnp.float32,
            )
            scores = scores * scale
            if masked:
                scores = scores + bias_ref[...]
            old_max = max_ref[rows, :]
            new_max = jnp.maximum(old_max, jnp.max(scores, axis=1, keepdims=True))
            carry = jnp.exp2(old_max - new_max)
            max_ref[rows, :] = new_max
            probs = jnp.exp2(scores - jnp.concatenate([new_max] * (width // HD), 1)).astype(jnp.bfloat16)
            mixed = jnp.dot(probs, values, preferred_element_type=jnp.float32)
            acc_ref[rows, :] = acc_ref[rows, :] * jnp.concatenate([carry, carry], 1) + mixed

    def one_block(step, src):
        @pl.when((src >= 0) & (src * tok + tok - 1 >= low) & (src <= my))
        def _():
            attend_blocks(step, src, 1, True)

    at = 0
    for count, mine, back in groups:
        newest = (my if mine else my ^ 1) - 2 * back
        if count == 1:
            one_block(at, newest)
        else:
            oldest = newest - 4 * (count - 1)
            whole = (oldest >= 0) & (oldest * tok >= high) & (newest < my)

            @pl.when(whole)
            def _(at=at, newest=newest, count=count):
                attend_blocks(at, newest, count, False)

            @pl.when(jnp.logical_not(whole))
            def _(at=at, newest=newest, count=count):
                def one_step(step, _):
                    one_block(at + step, newest - 4 * step)
                    return 0

                lax.fori_loop(0, count, one_step, 0)

        at += count
    if final:
        for h in range(GROUPS):
            acc = acc_ref[pl.ds(h * tok, tok), :]
            out_ref[:, h * HD : (h + 1) * HD] = (acc[:, :HD] / acc[:, HD:]).astype(jnp.bfloat16)


def attend(common, pieces, groups, state=None, final=False):
    query = common[-1]
    tok = query.shape[0]
    counts = tuple(piece.shape[0] // tok for piece in pieces)
    vmem, smem = pl.BlockSpec(memory_space=pltpu.VMEM), pl.BlockSpec(memory_space=pltpu.SMEM)
    state_shape = (
        jax.ShapeDtypeStruct((GROUPS * tok, 2 * HD), jnp.float32),
        jax.ShapeDtypeStruct((GROUPS * tok, HD), jnp.float32),
    )
    scratch = [
        pltpu.VMEM((tok, tok), jnp.float32),
        pltpu.VMEM((sum(counts) * tok, 2 * HD), jnp.bfloat16),
        pltpu.SemaphoreType.DMA((len(counts),)),
    ]
    out_shape = state_shape
    if final:
        out_shape += (jax.ShapeDtypeStruct((tok, GROUPS * HD), jnp.bfloat16),)
    flops = sum(counts) * GROUPS * tok * tok * HD * 4
    return pl.pallas_call(
        functools.partial(attend_kernel, counts, groups, state is None, final),
        out_shape=out_shape,
        in_specs=[smem] * 4
        + [vmem] * 2
        + [pl.BlockSpec(memory_space=pl.ANY)] * len(pieces)
        + [vmem] * (0 if state is None else 2),
        out_specs=(vmem,) * len(out_shape),
        scratch_shapes=scratch,
        input_output_aliases={} if state is None else {6 + len(pieces): 0, 7 + len(pieces): 1},
        compiler_params=pltpu.CompilerParams(vmem_limit_bytes=40 << 20),
        cost_estimate=pl.CostEstimate(flops=10 * flops, bytes_accessed=4 << 20, transcendentals=0),
    )(*common, *pieces, *(state or ()))


def local(query, keys_values, doc_start, scale_index, scale_table, out_weight):
    tok = query.shape[0]
    ctx_count = lax.axis_size("ctx")
    my = lax.axis_index("ctx").astype(jnp.int32)
    starts = jnp.broadcast_to(doc_start[:, None], (tok, HD))
    common = (my[None], doc_start, scale_index, scale_table, starts, query)

    def shifted(block, distance):
        return lax.ppermute(block, "ctx", [(i, i + distance) for i in range(ctx_count - distance)])

    def swapped(block):
        return lax.ppermute(block, "ctx", [(i, i ^ 1) for i in range(ctx_count)])

    def after(block, *others):
        return lax.optimization_barrier((block, *others))[0]

    from_2 = shifted(keys_values, 4)
    from_4 = shifted(from_2, 4)
    from_6 = shifted(from_4, 4)
    from_8 = shifted(from_6, 4)
    from_02 = jnp.concatenate([keys_values, from_2])
    from_13 = shifted(from_02, 2)
    from_46 = jnp.concatenate([from_4, from_6])
    from_57 = shifted(from_46, 2)
    other_1302 = swapped(jnp.concatenate([from_13, from_02]))
    state = attend(common, [keys_values, from_2], ((1, True, 0), (1, True, 2)))
    groups = ((2, True, 1), (2, True, 4), (2, False, 1), (1, False, 0), (1, False, 2))
    state = attend(common, [from_13, from_46, other_1302], groups, state)
    other_46857 = swapped(jnp.concatenate([from_46, from_8, after(from_57, *state)]))
    state = attend(common, [from_57, from_8], ((2, True, 5), (1, True, 8)), state)
    _, _, attn = attend(common, [other_46857], ((3, False, 4), (2, False, 5)), state, True)
    shares = lax.axis_size("kvh")
    partial = jnp.dot(attn, out_weight, preferred_element_type=jnp.float32).astype(jnp.bfloat16)
    pieces = lax.all_to_all(partial.reshape(shares, tok // shares, -1), "kvh", 0, 0)
    return jnp.sum(pieces.astype(jnp.float32), axis=0).astype(jnp.bfloat16)


def solution(mesh):
    placed = (P("ctx", "kvh"), P("ctx", "kvh"), P("ctx"), P(), P(None, "kvh"), P("kvh", None))
    return jax.shard_map(
        local, mesh=mesh, in_specs=placed, out_specs=P(("ctx", "kvh"), None), check_vma=False
    )
```

```python
import functools
import math

import jax
import jax.numpy as jnp
from jax import lax
from jax.experimental import pallas as pl
from jax.experimental.pallas import tpu as pltpu
from jax.sharding import PartitionSpec as P

H = 32
KVH = 8
HD = 128
SBLK = 128
GROUPS = H // KVH
NEG = -1e30
FACTOR = math.log2(math.e) / math.sqrt(HD)
SAFE = 80.0


def attend_kernel(
    counts, plan, first, final, my_ref, doc_ref, index_ref, table_ref, norm_ref, starts_ref, query_ref, *rest
):
    pieces, rest = rest[: len(counts)], rest[len(counts) :]
    if not first:
        rest = rest[2:]
    acc_ref, max_ref, *rest = rest
    if final:
        out_ref, *rest = rest
    bias_ref, held, src_ref, sems = rest
    tok = query_ref.shape[0]
    parts = tok // SBLK
    flag_row = GROUPS * tok
    blocks = len(plan)
    copies = []
    at = 0
    for i, count in enumerate(counts):
        copies.append(pltpu.make_async_copy(pieces[i], held.at[pl.ds(at * tok, count * tok)], sems.at[i]))
        copies[-1].start()
        at += count
    my, low, high = my_ref[0], doc_ref[0], doc_ref[tok - 1]
    for step, (mine, back, crossed) in enumerate(plan):
        src = (my if mine else my ^ 1) - 2 * back
        if crossed:
            src = src - 2 * (my & 2)
        src_ref[step] = src
    if blocks % 2:
        src_ref[blocks] = -1
        held[pl.ds(blocks * tok, tok), :] = jnp.zeros((tok, 2 * HD), held.dtype)
    if first:
        acc_ref[...] = jnp.zeros_like(acc_ref)
    for copy in copies:
        copy.wait()

    def scale_row(step, t):
        return index_ref[jnp.clip(src_ref[step], 0, my) * parts + t]

    def widest(step, most):
        for t in range(parts):
            rows = pl.ds(pl.multiple_of(step * tok + t * SBLK, SBLK), SBLK)
            key = held[rows, :HD].astype(jnp.float32)
            scale = table_ref[scale_row(step, t), 0] * FACTOR
            most = jnp.maximum(most, jnp.sum(key * key, axis=1, keepdims=True) * (scale * scale))
        return most

    most = lax.fori_loop(0, blocks, widest, jnp.zeros((SBLK, 1), jnp.float32))
    small = jnp.max(most) * norm_ref[0] <= SAFE * SAFE
    if first:
        max_ref[...] = jnp.full(max_ref.shape, jnp.where(small, 0.0, NEG), jnp.float32)
    else:
        small = small & (max_ref[flag_row, 0] > 0.0)
    max_ref[pl.ds(flag_row, 8), :] = jnp.full((8, HD), jnp.where(small, 1.0, 0.0), jnp.float32)

    def attend_pair(step, masked, shifted):
        key_scales, value_scales = [], []
        for t in range(2 * parts):
            row = scale_row(step + t // parts, t % parts)
            key_scales.append(jnp.full((1, SBLK), table_ref[row, 0] * FACTOR, jnp.float32))
            value_scales.append(jnp.full((SBLK, HD), table_ref[row, 1], jnp.float32))
        scale = jnp.concatenate(key_scales, 1)
        kv_rows = pl.ds(pl.multiple_of(step * tok, tok), 2 * tok)
        keys = held[kv_rows, :HD]
        values = held[kv_rows, HD:].astype(jnp.float32) * jnp.concatenate(value_scales, 0)
        values = jnp.concatenate([values.astype(jnp.bfloat16), jnp.ones((2 * tok, HD), jnp.bfloat16)], 1)
        if masked:
            column = lax.broadcasted_iota(jnp.int32, (tok, tok), 1)
            last = my * tok + lax.broadcasted_iota(jnp.int32, (tok, tok), 0)
            starts = jnp.concatenate([starts_ref[...]] * (tok // HD), 1)
            for i in range(2):
                key_pos = src_ref[step + i] * tok + column
                seen = (key_pos >= starts) & (key_pos <= last)
                bias_ref[:, i * tok : (i + 1) * tok] = jnp.where(seen, 0.0, NEG)
        for h in range(GROUPS):
            rows = pl.ds(h * tok, tok)
            scores = lax.dot_general(
                query_ref[:, h * HD : (h + 1) * HD],
                keys,
                (((1,), (1,)), ((), ())),
                preferred_element_type=jnp.float32,
            )
            scores = scores * scale
            if masked:
                scores = scores + bias_ref[...]
            if shifted:
                old_max = max_ref[rows, :]
                new_max = jnp.maximum(old_max, jnp.max(scores, axis=1, keepdims=True))
                carry = jnp.exp2(old_max - new_max)
                max_ref[rows, :] = new_max
                scores = scores - jnp.concatenate([new_max] * (2 * tok // HD), 1)
                acc_ref[rows, :] = acc_ref[rows, :] * jnp.concatenate([carry, carry], 1)
            probs = jnp.exp2(scores).astype(jnp.bfloat16)
            acc_ref[rows, :] += jnp.dot(probs, values, preferred_element_type=jnp.float32)

    def one_pair(pair, _):
        step = 2 * pair
        seen, whole = jnp.bool_(False), jnp.bool_(True)
        for i in range(2):
            src = src_ref[step + i]
            seen = seen | ((src >= 0) & (src * tok + tok - 1 >= low) & (src <= my))
            whole = whole & (src >= 0) & (src * tok >= high) & (src < my)

        @pl.when(seen & small & whole)
        def _():
            attend_pair(step, False, False)

        @pl.when(seen & small & jnp.logical_not(whole))
        def _():
            attend_pair(step, True, False)

        @pl.when(seen & jnp.logical_not(small))
        def _():
            attend_pair(step, True, True)

        return 0

    lax.fori_loop(0, (blocks + 1) // 2, one_pair, 0)
    if final:
        for h in range(GROUPS):
            acc = acc_ref[pl.ds(h * tok, tok), :]
            out_ref[:, h * HD : (h + 1) * HD] = (acc[:, :HD] / acc[:, HD:]).astype(jnp.bfloat16)


def attend(common, pieces, plan, state=None, final=False):
    query = common[-1]
    tok = query.shape[0]
    counts = tuple(piece.shape[0] // tok for piece in pieces)
    blocks = sum(counts)
    assert blocks == len(plan)
    even = blocks + blocks % 2
    vmem, smem = pl.BlockSpec(memory_space=pltpu.VMEM), pl.BlockSpec(memory_space=pltpu.SMEM)
    out_shape = (
        jax.ShapeDtypeStruct((GROUPS * tok, 2 * HD), jnp.float32),
        jax.ShapeDtypeStruct((GROUPS * tok + 8, HD), jnp.float32),
    )
    if final:
        out_shape += (jax.ShapeDtypeStruct((tok, GROUPS * HD), jnp.bfloat16),)
    flops = blocks * GROUPS * tok * tok * HD * 4
    return pl.pallas_call(
        functools.partial(attend_kernel, counts, plan, state is None, final),
        out_shape=out_shape,
        in_specs=[smem] * 5
        + [vmem] * 2
        + [pl.BlockSpec(memory_space=pl.ANY)] * len(pieces)
        + [vmem] * (0 if state is None else 2),
        out_specs=(vmem,) * len(out_shape),
        scratch_shapes=[
            pltpu.VMEM((tok, 2 * tok), jnp.float32),
            pltpu.VMEM((even * tok, 2 * HD), jnp.bfloat16),
            pltpu.SMEM((even,), jnp.int32),
            pltpu.SemaphoreType.DMA((len(counts),)),
        ],
        input_output_aliases={} if state is None else {7 + len(pieces): 0, 8 + len(pieces): 1},
        compiler_params=pltpu.CompilerParams(vmem_limit_bytes=40 << 20),
        cost_estimate=pl.CostEstimate(flops=10 * flops, bytes_accessed=4 << 20, transcendentals=0),
    )(*common, *pieces, *(state or ()))


def local(query, keys_values, doc_start, scale_index, scale_table, out_weight):
    tok = query.shape[0]
    ctx_count = lax.axis_size("ctx")
    my = lax.axis_index("ctx").astype(jnp.int32)
    starts = jnp.broadcast_to(doc_start[:, None], (tok, HD))
    squares = jnp.square(query.astype(jnp.float32)).reshape(tok, GROUPS, HD)
    norm = jnp.max(jnp.sum(squares, axis=2))
    common = (my[None], doc_start, scale_index, scale_table, norm[None], starts, query)

    def shifted(block, distance):
        return lax.ppermute(block, "ctx", [(i, i + distance) for i in range(ctx_count - distance)])

    def swapped(block):
        return lax.ppermute(block, "ctx", [(i, i ^ 1) for i in range(ctx_count)])

    def crossed(block):
        return lax.ppermute(block, "ctx", [(i, i ^ 2) for i in range(ctx_count)])

    def after(block, *others):
        return lax.optimization_barrier((block, *others))[0]

    def own(*back):
        return tuple((True, k, False) for k in back)

    def others(plan):
        return tuple((False, k, cross) for _, k, cross in plan)

    from_2 = shifted(keys_values, 4)
    from_02 = jnp.concatenate([keys_values, from_2])
    cross_02 = crossed(from_02)
    from_4 = shifted(from_2, 4)
    from_6 = shifted(from_4, 4)
    from_46 = jnp.concatenate([from_4, from_6])
    cross_46 = crossed(from_46)
    from_8 = shifted(from_6, 4)
    last = [(i, i + 2) for i in range(ctx_count - 2) if i & 2]
    from_7 = lax.ppermute(from_6, "ctx", last)
    plan_02, plan_46, plan_8 = own(0, 2), own(4, 6), own(8)
    cplan_02, cplan_46, cplan_7 = [tuple((True, k, True) for k in ks) for ks in ((-1, 1), (3, 5), (7,))]

    swap_02 = swapped(jnp.concatenate([from_02, cross_02]))
    state = attend(common, [keys_values, from_2], plan_02)
    plan = cplan_02 + plan_46 + others(plan_02 + cplan_02)
    state = attend(common, [cross_02, from_46, swap_02], plan, state)
    swap_46 = swapped(jnp.concatenate([from_46, from_8, from_7, after(cross_46, *state)]))
    state = attend(common, [cross_46, from_8, from_7], cplan_46 + plan_8 + cplan_7, state)
    plan = others(plan_46 + plan_8 + cplan_7 + cplan_46)
    _, _, attn = attend(common, [swap_46], plan, state, True)
    shares = lax.axis_size("kvh")
    partial = jnp.dot(attn, out_weight, preferred_element_type=jnp.float32).astype(jnp.bfloat16)
    pieces = lax.all_to_all(partial.reshape(shares, tok // shares, -1), "kvh", 0, 0)
    return jnp.sum(pieces.astype(jnp.float32), axis=0).astype(jnp.bfloat16)


def solution(mesh):
    placed = (P("ctx", "kvh"), P("ctx", "kvh"), P("ctx"), P(), P(None, "kvh"), P("kvh", None))
    return jax.shard_map(
        local, mesh=mesh, in_specs=placed, out_specs=P(("ctx", "kvh"), None), check_vma=False
    )
```

```python
import functools
import math

import jax
import jax.numpy as jnp
from jax import lax
from jax.experimental import pallas as pl
from jax.experimental.pallas import tpu as pltpu
from jax.sharding import PartitionSpec as P

H = 32
KVH = 8
HD = 128
SBLK = 128
GROUPS = H // KVH
NEG = -1e30
FACTOR = math.log2(math.e) / math.sqrt(HD)
SAFE = 80.0


def attend_kernel(
    counts, plan, first, final, my_ref, doc_ref, index_ref, table_ref, norm_ref, starts_ref, query_ref, *rest
):
    pieces, rest = rest[: len(counts)], rest[len(counts) :]
    if not first:
        rest = rest[2:]
    acc_ref, max_ref, *rest = rest
    if final:
        out_ref, *rest = rest
    bias_ref, held, src_ref, sems = rest
    tok = query_ref.shape[0]
    parts = tok // SBLK
    flag_row = GROUPS * tok
    blocks = len(plan)
    copies = []
    at = 0
    for i, count in enumerate(counts):
        copies.append(pltpu.make_async_copy(pieces[i], held.at[pl.ds(at * tok, count * tok)], sems.at[i]))
        copies[-1].start()
        at += count
    my, low, high = my_ref[0], doc_ref[0], doc_ref[tok - 1]
    for step, (mine, back, crossed) in enumerate(plan):
        src = (my if mine else my ^ 1) - 2 * back
        if crossed:
            src = src - 2 * (my & 2)
        src_ref[step] = src
    if blocks % 2:
        src_ref[blocks] = -1
        held[pl.ds(blocks * tok, tok), :] = jnp.zeros((tok, 2 * HD), held.dtype)
    if first:
        acc_ref[...] = jnp.zeros_like(acc_ref)
    for copy in copies:
        copy.wait()

    def scale_row(step, t):
        return index_ref[jnp.clip(src_ref[step], 0, my) * parts + t]

    ones = jnp.ones((HD, HD), jnp.bfloat16)

    def widest(step, most):
        key = held[pl.ds(pl.multiple_of(step * tok, tok), tok), :HD]
        squares = jnp.dot(key * key, ones, preferred_element_type=jnp.float32)
        for t in range(parts):
            scale = table_ref[0, scale_row(step, t)] * FACTOR
            most = jnp.maximum(most, squares[t * SBLK : (t + 1) * SBLK] * (scale * scale))
        return most

    most = lax.fori_loop(0, blocks, widest, jnp.zeros((SBLK, HD), jnp.float32))
    small = jnp.max(most) * norm_ref[0] <= SAFE * SAFE
    if first:
        max_ref[...] = jnp.full(max_ref.shape, jnp.where(small, 0.0, NEG), jnp.float32)
    else:
        small = small & (max_ref[flag_row, 0] > 0.0)
    max_ref[pl.ds(flag_row, 8), :] = jnp.full((8, HD), jnp.where(small, 1.0, 0.0), jnp.float32)

    def attend_pair(step, masked, shifted):
        key_scales, value_scales = [], []
        for t in range(2 * parts):
            row = scale_row(step + t // parts, t % parts)
            key_scales.append(jnp.full((1, SBLK), table_ref[0, row] * FACTOR, jnp.float32))
            value_scales.append(jnp.full((SBLK, HD), table_ref[1, row], jnp.float32))
        scale = jnp.concatenate(key_scales, 1)
        kv_rows = pl.ds(pl.multiple_of(step * tok, tok), 2 * tok)
        keys = held[kv_rows, :HD]
        values = held[kv_rows, HD:].astype(jnp.float32) * jnp.concatenate(value_scales, 0)
        values = jnp.concatenate([values.astype(jnp.bfloat16), jnp.ones((2 * tok, HD), jnp.bfloat16)], 1)
        if masked:
            column = lax.broadcasted_iota(jnp.int32, (tok, tok), 1)
            last = my * tok + lax.broadcasted_iota(jnp.int32, (tok, tok), 0)
            starts = jnp.concatenate([starts_ref[...]] * (tok // HD), 1)
            for i in range(2):
                key_pos = src_ref[step + i] * tok + column
                seen = (key_pos >= starts) & (key_pos <= last)
                bias_ref[:, i * tok : (i + 1) * tok] = jnp.where(seen, 0.0, NEG)
        for h in range(GROUPS):
            rows = pl.ds(h * tok, tok)
            scores = lax.dot_general(
                query_ref[:, h * HD : (h + 1) * HD],
                keys,
                (((1,), (1,)), ((), ())),
                preferred_element_type=jnp.float32,
            )
            scores = scores * scale
            if masked:
                scores = scores + bias_ref[...]
            if shifted:
                old_max = max_ref[rows, :]
                new_max = jnp.maximum(old_max, jnp.max(scores, axis=1, keepdims=True))
                carry = jnp.exp2(old_max - new_max)
                max_ref[rows, :] = new_max
                scores = scores - jnp.concatenate([new_max] * (2 * tok // HD), 1)
                acc_ref[rows, :] = acc_ref[rows, :] * jnp.concatenate([carry, carry], 1)
            probs = jnp.exp2(scores).astype(jnp.bfloat16)
            acc_ref[rows, :] += jnp.dot(probs, values, preferred_element_type=jnp.float32)

    def one_pair(pair, _):
        step = 2 * pair
        seen, whole = jnp.bool_(False), jnp.bool_(True)
        for i in range(2):
            src = src_ref[step + i]
            seen = seen | ((src >= 0) & (src * tok + tok - 1 >= low) & (src <= my))
            whole = whole & (src >= 0) & (src * tok >= high) & (src < my)

        @pl.when(seen & small & whole)
        def _():
            attend_pair(step, False, False)

        @pl.when(seen & small & jnp.logical_not(whole))
        def _():
            attend_pair(step, True, False)

        @pl.when(seen & jnp.logical_not(small))
        def _():
            attend_pair(step, True, True)

        return 0

    lax.fori_loop(0, (blocks + 1) // 2, one_pair, 0)
    if final:
        for h in range(GROUPS):
            acc = acc_ref[pl.ds(h * tok, tok), :]
            out_ref[:, h * HD : (h + 1) * HD] = (acc[:, :HD] / acc[:, HD:]).astype(jnp.bfloat16)


def attend(common, pieces, plan, state=None, final=False):
    query = common[-1]
    tok = query.shape[0]
    counts = tuple(piece.shape[0] // tok for piece in pieces)
    blocks = sum(counts)
    assert blocks == len(plan)
    even = blocks + blocks % 2
    vmem, smem = pl.BlockSpec(memory_space=pltpu.VMEM), pl.BlockSpec(memory_space=pltpu.SMEM)
    out_shape = (
        jax.ShapeDtypeStruct((GROUPS * tok, 2 * HD), jnp.float32),
        jax.ShapeDtypeStruct((GROUPS * tok + 8, HD), jnp.float32),
    )
    if final:
        out_shape += (jax.ShapeDtypeStruct((tok, GROUPS * HD), jnp.bfloat16),)
    flops = blocks * GROUPS * tok * tok * HD * 4
    return pl.pallas_call(
        functools.partial(attend_kernel, counts, plan, state is None, final),
        out_shape=out_shape,
        in_specs=[smem] * 5
        + [vmem] * 2
        + [pl.BlockSpec(memory_space=pl.ANY)] * len(pieces)
        + [vmem] * (0 if state is None else 2),
        out_specs=(vmem,) * len(out_shape),
        scratch_shapes=[
            pltpu.VMEM((tok, 2 * tok), jnp.float32),
            pltpu.VMEM((even * tok, 2 * HD), jnp.bfloat16),
            pltpu.SMEM((even,), jnp.int32),
            pltpu.SemaphoreType.DMA((len(counts),)),
        ],
        input_output_aliases={} if state is None else {7 + len(pieces): 0, 8 + len(pieces): 1},
        compiler_params=pltpu.CompilerParams(vmem_limit_bytes=40 << 20),
        cost_estimate=pl.CostEstimate(flops=10 * flops, bytes_accessed=4 << 20, transcendentals=0),
    )(*common, *pieces, *(state or ()))


def local(query, keys_values, doc_start, scale_index, scale_table, out_weight):
    tok = query.shape[0]
    ctx_count = lax.axis_size("ctx")
    my = lax.axis_index("ctx").astype(jnp.int32)
    starts = jnp.broadcast_to(doc_start[:, None], (tok, HD))
    squares = jnp.square(query.astype(jnp.float32)).reshape(tok, GROUPS, HD)
    norm = jnp.max(jnp.sum(squares, axis=2))
    common = (my[None], doc_start, scale_index, scale_table.T, norm[None], starts, query)

    def shifted(block, distance):
        return lax.ppermute(block, "ctx", [(i, i + distance) for i in range(ctx_count - distance)])

    def swapped(block):
        return lax.ppermute(block, "ctx", [(i, i ^ 1) for i in range(ctx_count)])

    def crossed(block):
        return lax.ppermute(block, "ctx", [(i, i ^ 2) for i in range(ctx_count)])

    def after(block, *others):
        return lax.optimization_barrier((block, *others))[0]

    def own(*back):
        return tuple((True, k, False) for k in back)

    def others(plan):
        return tuple((False, k, cross) for _, k, cross in plan)

    from_2 = shifted(keys_values, 4)
    from_02 = jnp.concatenate([keys_values, after(from_2, norm, starts)])
    from_46 = shifted(from_02, 8)
    cross_02 = crossed(from_02)
    last = [(i, i + 2) for i in range(ctx_count - 2) if i & 2]
    plan_02, plan_46, plan_8 = own(0, 2), own(4, 6), own(8)
    cplan_02, cplan_46, cplan_7 = [tuple((True, k, True) for k in ks) for ks in ((-1, 1), (3, 5), (7,))]

    swap_02 = swapped(jnp.concatenate([from_02, cross_02]))
    state = attend(common, [from_02, cross_02], plan_02 + cplan_02)
    from_46 = after(from_46, *state)
    from_6 = from_46[tok:]
    cross_46 = crossed(from_46)
    from_8 = shifted(from_6, 4)
    from_7 = lax.ppermute(from_6, "ctx", last)
    plan = plan_46 + others(plan_02 + cplan_02)
    state = attend(common, [from_46, swap_02], plan, state)
    swap_46 = swapped(jnp.concatenate([from_46, from_8, from_7, after(cross_46, *state)]))
    state = attend(common, [cross_46, from_8, from_7], cplan_46 + plan_8 + cplan_7, state)
    plan = others(plan_46 + plan_8 + cplan_7 + cplan_46)
    _, _, attn = attend(common, [swap_46], plan, state, True)
    shares = lax.axis_size("kvh")
    partial = jnp.dot(attn, out_weight, preferred_element_type=jnp.float32).astype(jnp.bfloat16)
    pieces = lax.all_to_all(partial.reshape(shares, tok // shares, -1), "kvh", 0, 0)
    return jnp.sum(pieces.astype(jnp.float32), axis=0).astype(jnp.bfloat16)


def solution(mesh):
    placed = (P("ctx", "kvh"), P("ctx", "kvh"), P("ctx"), P(), P(None, "kvh"), P("kvh", None))
    return jax.shard_map(
        local, mesh=mesh, in_specs=placed, out_specs=P(("ctx", "kvh"), None), check_vma=False
    )
```

```python
import functools
import math

import jax
import jax.numpy as jnp
from jax import lax
from jax.experimental import pallas as pl
from jax.experimental.pallas import tpu as pltpu
from jax.sharding import PartitionSpec as P

H = 32
KVH = 8
HD = 128
SBLK = 128
GROUPS = H // KVH
NEG = -1e30
FACTOR = math.log2(math.e) / math.sqrt(HD)
SAFE = 80.0


def attend_kernel(
    counts, plan, first, final, my_ref, doc_ref, index_ref, table_ref, norm_ref, starts_ref, query_ref, *rest
):
    pieces, rest = rest[: len(counts)], rest[len(counts) :]
    if not first:
        rest = rest[2:]
    acc_ref, max_ref, *rest = rest
    if final:
        out_ref, *rest = rest
    bias_ref, held, src_ref, sems = rest
    tok = query_ref.shape[0]
    parts = tok // SBLK
    flag_row = GROUPS * tok
    blocks = len(plan)
    copies = []
    at = 0
    for i, count in enumerate(counts):
        copies.append(pltpu.make_async_copy(pieces[i], held.at[pl.ds(at * tok, count * tok)], sems.at[i]))
        copies[-1].start()
        at += count
    my, low, high = my_ref[0], doc_ref[0], doc_ref[tok - 1]
    for step, (mine, back, crossed) in enumerate(plan):
        src = (my if mine else my ^ 1) - 2 * back
        if crossed:
            src = src - 2 * (my & 2)
        src_ref[step] = src
    if blocks % 2:
        src_ref[blocks] = -1
        held[pl.ds(blocks * tok, tok), :] = jnp.zeros((tok, 2 * HD), held.dtype)
    if first:
        acc_ref[...] = jnp.zeros_like(acc_ref)
    for copy in copies:
        copy.wait()

    def scale_row(step, t):
        return index_ref[jnp.clip(src_ref[step], 0, my) * parts + t]

    ones = jnp.ones((HD, HD), jnp.bfloat16)

    def widest(step, most):
        key = held[pl.ds(pl.multiple_of(step * tok, tok), tok), :HD]
        squares = jnp.dot(key * key, ones, preferred_element_type=jnp.float32)
        for t in range(parts):
            scale = table_ref[0, scale_row(step, t)] * FACTOR
            most = jnp.maximum(most, squares[t * SBLK : (t + 1) * SBLK] * (scale * scale))
        return most

    most = lax.fori_loop(0, blocks, widest, jnp.zeros((SBLK, HD), jnp.float32))
    small = jnp.max(most) * norm_ref[0] <= SAFE * SAFE
    if first:
        max_ref[...] = jnp.full(max_ref.shape, jnp.where(small, 0.0, NEG), jnp.float32)
    else:
        small = small & (max_ref[flag_row, 0] > 0.0)
    max_ref[pl.ds(flag_row, 8), :] = jnp.full((8, HD), jnp.where(small, 1.0, 0.0), jnp.float32)

    def attend_pair(step, masked, shifted):
        key_scales, value_scales = [], []
        for t in range(2 * parts):
            row = scale_row(step + t // parts, t % parts)
            key_scales.append(jnp.full((1, SBLK), table_ref[0, row] * FACTOR, jnp.float32))
            value_scales.append(jnp.full((SBLK, HD), table_ref[1, row], jnp.float32))
        scale = jnp.concatenate(key_scales, 1)
        kv_rows = pl.ds(pl.multiple_of(step * tok, tok), 2 * tok)
        keys = held[kv_rows, :HD]
        values = held[kv_rows, HD:].astype(jnp.float32) * jnp.concatenate(value_scales, 0)
        values = jnp.concatenate([values.astype(jnp.bfloat16), jnp.ones((2 * tok, HD), jnp.bfloat16)], 1)
        if masked:
            column = lax.broadcasted_iota(jnp.int32, (tok, tok), 1)
            last = my * tok + lax.broadcasted_iota(jnp.int32, (tok, tok), 0)
            starts = jnp.concatenate([starts_ref[...]] * (tok // HD), 1)
            for i in range(2):
                key_pos = src_ref[step + i] * tok + column
                seen = (key_pos >= starts) & (key_pos <= last)
                bias_ref[:, i * tok : (i + 1) * tok] = jnp.where(seen, 0.0, NEG)
        for h in range(GROUPS):
            rows = pl.ds(h * tok, tok)
            scores = lax.dot_general(
                query_ref[:, h * HD : (h + 1) * HD],
                keys,
                (((1,), (1,)), ((), ())),
                preferred_element_type=jnp.float32,
            )
            scores = scores * scale
            if masked:
                scores = scores + bias_ref[...]
            if shifted:
                old_max = max_ref[rows, :]
                new_max = jnp.maximum(old_max, jnp.max(scores, axis=1, keepdims=True))
                carry = jnp.exp2(old_max - new_max)
                max_ref[rows, :] = new_max
                scores = scores - jnp.concatenate([new_max] * (2 * tok // HD), 1)
                acc_ref[rows, :] = acc_ref[rows, :] * jnp.concatenate([carry, carry], 1)
            probs = jnp.exp2(scores).astype(jnp.bfloat16)
            acc_ref[rows, :] += jnp.dot(probs, values, preferred_element_type=jnp.float32)

    def one_pair(pair, _):
        step = 2 * pair
        seen, whole = jnp.bool_(False), jnp.bool_(True)
        for i in range(2):
            src = src_ref[step + i]
            seen = seen | ((src >= 0) & (src * tok + tok - 1 >= low) & (src <= my))
            whole = whole & (src >= 0) & (src * tok >= high) & (src < my)

        @pl.when(seen & small & whole)
        def _():
            attend_pair(step, False, False)

        @pl.when(seen & small & jnp.logical_not(whole))
        def _():
            attend_pair(step, True, False)

        @pl.when(seen & jnp.logical_not(small))
        def _():
            attend_pair(step, True, True)

        return 0

    lax.fori_loop(0, (blocks + 1) // 2, one_pair, 0)
    if final:
        for h in range(GROUPS):
            acc = acc_ref[pl.ds(h * tok, tok), :]
            out_ref[:, h * HD : (h + 1) * HD] = (acc[:, :HD] / acc[:, HD:]).astype(jnp.bfloat16)


def attend(common, pieces, plan, state=None, final=False):
    query = common[-1]
    tok = query.shape[0]
    counts = tuple(piece.shape[0] // tok for piece in pieces)
    blocks = sum(counts)
    assert blocks == len(plan)
    even = blocks + blocks % 2
    vmem, smem = pl.BlockSpec(memory_space=pltpu.VMEM), pl.BlockSpec(memory_space=pltpu.SMEM)
    out_shape = (
        jax.ShapeDtypeStruct((GROUPS * tok, 2 * HD), jnp.float32),
        jax.ShapeDtypeStruct((GROUPS * tok + 8, HD), jnp.float32),
    )
    if final:
        out_shape += (jax.ShapeDtypeStruct((tok, GROUPS * HD), jnp.bfloat16),)
    flops = blocks * GROUPS * tok * tok * HD * 4
    return pl.pallas_call(
        functools.partial(attend_kernel, counts, plan, state is None, final),
        out_shape=out_shape,
        in_specs=[smem] * 5
        + [vmem] * 2
        + [pl.BlockSpec(memory_space=pl.ANY)] * len(pieces)
        + [vmem] * (0 if state is None else 2),
        out_specs=(vmem,) * len(out_shape),
        scratch_shapes=[
            pltpu.VMEM((tok, 2 * tok), jnp.float32),
            pltpu.VMEM((even * tok, 2 * HD), jnp.bfloat16),
            pltpu.SMEM((even,), jnp.int32),
            pltpu.SemaphoreType.DMA((len(counts),)),
        ],
        input_output_aliases={} if state is None else {7 + len(pieces): 0, 8 + len(pieces): 1},
        compiler_params=pltpu.CompilerParams(vmem_limit_bytes=40 << 20),
        cost_estimate=pl.CostEstimate(flops=10 * flops, bytes_accessed=4 << 20, transcendentals=0),
    )(*common, *pieces, *(state or ()))


def local(query, keys_values, doc_start, scale_index, scale_table, out_weight):
    tok = query.shape[0]
    ctx_count = lax.axis_size("ctx")
    my = lax.axis_index("ctx").astype(jnp.int32)
    starts = jnp.broadcast_to(doc_start[:, None], (tok, HD))
    squares = jnp.square(query.astype(jnp.float32)).reshape(tok, GROUPS, HD)
    norm = jnp.max(jnp.sum(squares, axis=2))
    common = (my[None], doc_start, scale_index, scale_table.T, norm[None], starts, query)

    def shifted(block, distance):
        return lax.ppermute(block, "ctx", [(i, i + distance) for i in range(ctx_count - distance)])

    def swapped(block):
        return lax.ppermute(block, "ctx", [(i, i ^ 1) for i in range(ctx_count)])

    def crossed(block):
        return lax.ppermute(block, "ctx", [(i, i ^ 2) for i in range(ctx_count)])

    def after(block, *others):
        return lax.optimization_barrier((block, *others))[0]

    def own(*back):
        return tuple((True, k, False) for k in back)

    def others(plan):
        return tuple((False, k, cross) for _, k, cross in plan)

    half = out_weight.shape[1] // 2
    side = (lax.axis_index("kvh") // 2) % 2
    pairs = [(k, k ^ 2) for k in range(lax.axis_size("kvh"))]
    own_weight = lax.dynamic_slice_in_dim(out_weight, side * half, half, 1)
    sent_weight = lax.dynamic_slice_in_dim(out_weight, (1 - side) * half, half, 1)
    pair_weight = lax.ppermute(sent_weight, "kvh", pairs)

    from_2 = shifted(keys_values, 4)
    from_02 = jnp.concatenate([keys_values, after(from_2, norm, starts)])
    from_46 = shifted(from_02, 8)
    cross_02 = crossed(from_02)
    last = [(i, i + 2) for i in range(ctx_count - 2) if i & 2]
    plan_02, plan_46, plan_8 = own(0, 2), own(4, 6), own(8)
    cplan_02, cplan_46, cplan_7 = [tuple((True, k, True) for k in ks) for ks in ((-1, 1), (3, 5), (7,))]

    swap_02 = swapped(jnp.concatenate([from_02, cross_02]))
    state = attend(common, [from_02, cross_02], plan_02 + cplan_02)
    from_46 = after(from_46, *state)
    from_6 = from_46[tok:]
    cross_46 = crossed(after(from_46, swap_02))
    from_8 = shifted(from_6, 4)
    from_7 = lax.ppermute(from_6, "ctx", last)
    plan = plan_46 + others(plan_02 + cplan_02)
    state = attend(common, [from_46, after(swap_02, pair_weight)], plan, state)
    swap_46 = swapped(jnp.concatenate([from_46, from_8, from_7, after(cross_46, *state)]))
    state = attend(common, [cross_46, from_8, from_7], cplan_46 + plan_8 + cplan_7, state)
    plan = others(plan_46 + plan_8 + cplan_7 + cplan_46)
    _, _, attn = attend(common, [swap_46], plan, state, True)
    shares = lax.axis_size("kvh")
    pair_attn = lax.ppermute(attn, "kvh", pairs)
    partial = jnp.dot(attn, own_weight, preferred_element_type=jnp.float32)
    partial = partial + jnp.dot(pair_attn, pair_weight, preferred_element_type=jnp.float32)
    partial = partial.astype(jnp.bfloat16).reshape(shares, tok // shares, half)
    pieces = lax.all_to_all(partial, "kvh", 0, 0)
    pieces = pieces.astype(jnp.float32).reshape(shares // 4, 2, 2, tok // shares, half)
    summed = jnp.sum(pieces, axis=(0, 2)).astype(jnp.bfloat16)
    return jnp.concatenate([summed[0], summed[1]], axis=1)


def solution(mesh):
    placed = (P("ctx", "kvh"), P("ctx", "kvh"), P("ctx"), P(), P(None, "kvh"), P("kvh", None))
    return jax.shard_map(
        local, mesh=mesh, in_specs=placed, out_specs=P(("ctx", "kvh"), None), check_vma=False
    )
```

```python
import functools
import math

import jax
import jax.numpy as jnp
from jax import lax
from jax.experimental import pallas as pl
from jax.experimental.pallas import tpu as pltpu
from jax.sharding import PartitionSpec as P

H = 32
KVH = 8
HD = 128
SBLK = 128
GROUPS = H // KVH
NEG = -1e30
FACTOR = math.log2(math.e) / math.sqrt(HD)
SAFE = 80.0


def attend_kernel(
    counts, plan, first, final, my_ref, doc_ref, index_ref, table_ref, norm_ref, starts_ref, query_ref, *rest
):
    pieces, rest = rest[: len(counts)], rest[len(counts) :]
    if not first:
        rest = rest[2:]
    acc_ref, max_ref, *rest = rest
    if final:
        out_ref, *rest = rest
    bias_ref, held, src_ref = rest
    tok = query_ref.shape[0]
    parts = tok // SBLK
    flag_row = GROUPS * tok
    blocks = len(plan)
    at = 0
    for piece, count in zip(pieces, counts):
        held[pl.ds(at * tok, count * tok), :] = piece[...]
        at += count
    my, low, high = my_ref[0], doc_ref[0], doc_ref[tok - 1]
    for step, (mine, back, crossed) in enumerate(plan):
        src = (my if mine else my ^ 1) - 2 * back
        if crossed:
            src = src - 2 * (my & 2)
        src_ref[step] = src
    if blocks % 2:
        src_ref[blocks] = -1
        held[pl.ds(blocks * tok, tok), :] = jnp.zeros((tok, 2 * HD), held.dtype)
    if first:
        acc_ref[...] = jnp.zeros_like(acc_ref)

    def scale_row(step, t):
        return index_ref[jnp.clip(src_ref[step], 0, my) * parts + t]

    ones = jnp.ones((HD, HD), jnp.bfloat16)

    most = jnp.zeros((SBLK, HD), jnp.float32)
    for step in range(blocks):
        key = held[pl.ds(step * tok, tok), :HD]
        squares = jnp.dot(key * key, ones, preferred_element_type=jnp.float32)
        for t in range(parts):
            scale = table_ref[0, scale_row(step, t)] * FACTOR
            most = jnp.maximum(most, squares[t * SBLK : (t + 1) * SBLK] * (scale * scale))
    small = jnp.max(most) * norm_ref[0] <= SAFE * SAFE
    if first:
        max_ref[...] = jnp.full(max_ref.shape, jnp.where(small, 0.0, NEG), jnp.float32)
    else:
        small = small & (max_ref[flag_row, 0] > 0.0)
    max_ref[pl.ds(flag_row, 8), :] = jnp.full((8, HD), jnp.where(small, 1.0, 0.0), jnp.float32)

    def attend_pair(step, masked, shifted):
        key_scales, value_scales = [], []
        for t in range(2 * parts):
            row = scale_row(step + t // parts, t % parts)
            key_scales.append(jnp.full((1, SBLK), table_ref[0, row] * FACTOR, jnp.float32))
            value_scales.append(jnp.full((SBLK, HD), table_ref[1, row], jnp.float32))
        scale = jnp.concatenate(key_scales, 1)
        kv_rows = pl.ds(pl.multiple_of(step * tok, tok), 2 * tok)
        keys = held[kv_rows, :HD]
        values = held[kv_rows, HD:].astype(jnp.float32) * jnp.concatenate(value_scales, 0)
        values = jnp.concatenate([values.astype(jnp.bfloat16), jnp.ones((2 * tok, HD), jnp.bfloat16)], 1)
        if masked:
            column = lax.broadcasted_iota(jnp.int32, (tok, tok), 1)
            last = my * tok + lax.broadcasted_iota(jnp.int32, (tok, tok), 0)
            starts = jnp.concatenate([starts_ref[...]] * (tok // HD), 1)
            for i in range(2):
                key_pos = src_ref[step + i] * tok + column
                seen = (key_pos >= starts) & (key_pos <= last)
                bias_ref[:, i * tok : (i + 1) * tok] = jnp.where(seen, 0.0, NEG)
        for h in range(GROUPS):
            rows = pl.ds(h * tok, tok)
            scores = lax.dot_general(
                query_ref[:, h * HD : (h + 1) * HD],
                keys,
                (((1,), (1,)), ((), ())),
                preferred_element_type=jnp.float32,
            )
            scores = scores * scale
            if masked:
                scores = scores + bias_ref[...]
            if shifted:
                old_max = max_ref[rows, :]
                new_max = jnp.maximum(old_max, jnp.max(scores, axis=1, keepdims=True))
                carry = jnp.exp2(old_max - new_max)
                max_ref[rows, :] = new_max
                scores = scores - jnp.concatenate([new_max] * (2 * tok // HD), 1)
                acc_ref[rows, :] = acc_ref[rows, :] * jnp.concatenate([carry, carry], 1)
            probs = jnp.exp2(scores).astype(jnp.bfloat16)
            acc_ref[rows, :] += jnp.dot(probs, values, preferred_element_type=jnp.float32)

    def one_pair(pair, _):
        step = 2 * pair
        seen, whole = jnp.bool_(False), jnp.bool_(True)
        for i in range(2):
            src = src_ref[step + i]
            seen = seen | ((src >= 0) & (src * tok + tok - 1 >= low) & (src <= my))
            whole = whole & (src >= 0) & (src * tok >= high) & (src < my)

        @pl.when(seen & small & whole)
        def _():
            attend_pair(step, False, False)

        @pl.when(seen & small & jnp.logical_not(whole))
        def _():
            attend_pair(step, True, False)

        @pl.when(seen & jnp.logical_not(small))
        def _():
            attend_pair(step, True, True)

        return 0

    lax.fori_loop(0, (blocks + 1) // 2, one_pair, 0)
    if final:
        for h in range(GROUPS):
            acc = acc_ref[pl.ds(h * tok, tok), :]
            out_ref[:, h * HD : (h + 1) * HD] = (acc[:, :HD] / acc[:, HD:]).astype(jnp.bfloat16)


def attend(common, pieces, plan, state=None, final=False):
    query = common[-1]
    tok = query.shape[0]
    counts = tuple(piece.shape[0] // tok for piece in pieces)
    blocks = sum(counts)
    assert blocks == len(plan)
    even = blocks + blocks % 2
    vmem, smem = pl.BlockSpec(memory_space=pltpu.VMEM), pl.BlockSpec(memory_space=pltpu.SMEM)
    out_shape = (
        jax.ShapeDtypeStruct((GROUPS * tok, 2 * HD), jnp.float32),
        jax.ShapeDtypeStruct((GROUPS * tok + 8, HD), jnp.float32),
    )
    if final:
        out_shape += (jax.ShapeDtypeStruct((tok, GROUPS * HD), jnp.bfloat16),)
    flops = blocks * GROUPS * tok * tok * HD * 4
    return pl.pallas_call(
        functools.partial(attend_kernel, counts, plan, state is None, final),
        out_shape=out_shape,
        in_specs=[smem] * 5
        + [vmem] * (2 + len(pieces))
        + [vmem] * (0 if state is None else 2),
        out_specs=(vmem,) * len(out_shape),
        scratch_shapes=[
            pltpu.VMEM((tok, 2 * tok), jnp.float32),
            pltpu.VMEM((even * tok, 2 * HD), jnp.bfloat16),
            pltpu.SMEM((even,), jnp.int32),
        ],
        input_output_aliases={} if state is None else {7 + len(pieces): 0, 8 + len(pieces): 1},
        compiler_params=pltpu.CompilerParams(vmem_limit_bytes=40 << 20),
        cost_estimate=pl.CostEstimate(flops=10 * flops, bytes_accessed=4 << 20, transcendentals=0),
    )(*common, *pieces, *(state or ()))


def local(query, keys_values, doc_start, scale_index, scale_table, out_weight):
    tok = query.shape[0]
    ctx_count = lax.axis_size("ctx")
    my = lax.axis_index("ctx").astype(jnp.int32)
    starts = jnp.broadcast_to(doc_start[:, None], (tok, HD))
    squares = jnp.square(query.astype(jnp.float32)).reshape(tok, GROUPS, HD)
    norm = jnp.max(jnp.sum(squares, axis=2))
    common = (my[None], doc_start, scale_index, scale_table.T, norm[None], starts, query)

    def shifted(block, distance):
        return lax.ppermute(block, "ctx", [(i, i + distance) for i in range(ctx_count - distance)])

    def swapped(block):
        return lax.ppermute(block, "ctx", [(i, i ^ 1) for i in range(ctx_count)])

    def crossed(block):
        return lax.ppermute(block, "ctx", [(i, i ^ 2) for i in range(ctx_count)])

    def after(block, *others):
        return lax.optimization_barrier((block, *others))[0]

    def own(*back):
        return tuple((True, k, False) for k in back)

    def others(plan):
        return tuple((False, k, cross) for _, k, cross in plan)

    from_2 = shifted(keys_values, 4)
    from_02 = jnp.concatenate([keys_values, after(from_2, norm, starts)])
    from_46 = shifted(from_02, 8)
    cross_02 = crossed(from_02)
    last = [(i, i + 2) for i in range(ctx_count - 2) if i & 2]
    plan_02, plan_46, plan_8 = own(0, 2), own(4, 6), own(8)
    cplan_02, cplan_46, cplan_7 = [tuple((True, k, True) for k in ks) for ks in ((-1, 1), (3, 5), (7,))]

    swap_02 = swapped(jnp.concatenate([from_02, cross_02]))
    state = attend(common, [from_02, cross_02], plan_02 + cplan_02)
    from_46 = after(from_46, *state)
    from_6 = from_46[tok:]
    cross_46 = crossed(after(from_46, swap_02))
    from_8 = shifted(from_6, 4)
    from_7 = lax.ppermute(from_6, "ctx", last)
    plan = plan_46 + others(plan_02 + cplan_02)
    state = attend(common, [from_46, swap_02], plan, state)
    swap_46 = swapped(jnp.concatenate([from_46, from_8, from_7, after(cross_46, *state)]))
    state = attend(common, [cross_46, from_8, from_7], cplan_46 + plan_8 + cplan_7, state)
    plan = others(plan_46 + plan_8 + cplan_7 + cplan_46)
    _, _, attn = attend(common, [swap_46], plan, state, True)
    shares = lax.axis_size("kvh")
    partial = jnp.dot(attn, out_weight, preferred_element_type=jnp.float32).astype(jnp.bfloat16)
    pieces = lax.all_to_all(partial.reshape(shares, tok // shares, -1), "kvh", 0, 0)
    return jnp.sum(pieces.astype(jnp.float32), axis=0).astype(jnp.bfloat16)


def solution(mesh):
    placed = (P("ctx", "kvh"), P("ctx", "kvh"), P("ctx"), P(), P(None, "kvh"), P("kvh", None))
    return jax.shard_map(
        local, mesh=mesh, in_specs=placed, out_specs=P(("ctx", "kvh"), None), check_vma=False
    )
```

```python
import functools
import math

import jax
import jax.numpy as jnp
from jax import lax
from jax.experimental import pallas as pl
from jax.experimental.pallas import tpu as pltpu
from jax.sharding import PartitionSpec as P

H = 32
KVH = 8
HD = 128
SBLK = 128
GROUPS = H // KVH
NEG = -1e30
FACTOR = math.log2(math.e) / math.sqrt(HD)
SAFE = 80.0


def attend_kernel(
    counts, plan, first, final, my_ref, doc_ref, index_ref, table_ref, norm_ref, starts_ref, query_ref, *rest
):
    pieces, rest = rest[: len(counts)], rest[len(counts) :]
    if not first:
        rest = rest[2:]
    acc_ref, max_ref, *rest = rest
    if final:
        out_ref, *rest = rest
    bias_ref, held, src_ref = rest
    tok = query_ref.shape[0]
    parts = tok // SBLK
    flag_row = GROUPS * tok
    blocks = len(plan)
    at = 0
    for piece, count in zip(pieces, counts):
        held[pl.ds(at * tok, count * tok), :] = piece[...]
        at += count
    my, low, high = my_ref[0], doc_ref[0], doc_ref[tok - 1]
    for step, (mine, back, crossed) in enumerate(plan):
        src = (my if mine else my ^ 1) - 2 * back
        if crossed:
            src = src - 2 * (my & 2)
        src_ref[step] = src
    if blocks % 2:
        src_ref[blocks] = -1
        held[pl.ds(blocks * tok, tok), :] = jnp.zeros((tok, 2 * HD), held.dtype)
    if first:
        acc_ref[...] = jnp.zeros_like(acc_ref)

    def scale_row(step, t):
        return index_ref[jnp.clip(src_ref[step], 0, my) * parts + t]

    ones = jnp.ones((HD, HD), jnp.bfloat16)

    most = jnp.zeros((SBLK, HD), jnp.float32)
    for step in range(blocks):
        key = held[pl.ds(step * tok, tok), :HD]
        squares = jnp.dot(key * key, ones, preferred_element_type=jnp.float32)
        for t in range(parts):
            scale = table_ref[0, scale_row(step, t)] * FACTOR
            most = jnp.maximum(most, squares[t * SBLK : (t + 1) * SBLK] * (scale * scale))
    small = jnp.max(most) * norm_ref[0] <= SAFE * SAFE
    if first:
        max_ref[...] = jnp.full(max_ref.shape, jnp.where(small, 0.0, NEG), jnp.float32)
    else:
        small = small & (max_ref[flag_row, 0] > 0.0)
    max_ref[pl.ds(flag_row, 8), :] = jnp.full((8, HD), jnp.where(small, 1.0, 0.0), jnp.float32)

    def attend_pair(step, masked, shifted):
        key_scales, value_scales = [], []
        for t in range(2 * parts):
            row = scale_row(step + t // parts, t % parts)
            key_scales.append(jnp.full((1, SBLK), table_ref[0, row] * FACTOR, jnp.float32))
            value_scales.append(jnp.full((SBLK, HD), table_ref[1, row], jnp.float32))
        scale = jnp.concatenate(key_scales, 1)
        kv_rows = pl.ds(pl.multiple_of(step * tok, tok), 2 * tok)
        keys = held[kv_rows, :HD]
        values = held[kv_rows, HD:].astype(jnp.float32) * jnp.concatenate(value_scales, 0)
        values = jnp.concatenate([values.astype(jnp.bfloat16), jnp.ones((2 * tok, HD), jnp.bfloat16)], 1)
        if masked:
            column = lax.broadcasted_iota(jnp.int32, (tok, tok), 1)
            last = my * tok + lax.broadcasted_iota(jnp.int32, (tok, tok), 0)
            starts = jnp.concatenate([starts_ref[...]] * (tok // HD), 1)
            for i in range(2):
                key_pos = src_ref[step + i] * tok + column
                seen = (key_pos >= starts) & (key_pos <= last)
                bias_ref[:, i * tok : (i + 1) * tok] = jnp.where(seen, 0.0, NEG)
        for h in range(GROUPS):
            rows = pl.ds(h * tok, tok)
            scores = lax.dot_general(
                query_ref[:, h * HD : (h + 1) * HD],
                keys,
                (((1,), (1,)), ((), ())),
                preferred_element_type=jnp.float32,
            )
            scores = scores * scale
            if masked:
                scores = scores + bias_ref[...]
            if shifted:
                old_max = max_ref[rows, :]
                new_max = jnp.maximum(old_max, jnp.max(scores, axis=1, keepdims=True))
                carry = jnp.exp2(old_max - new_max)
                max_ref[rows, :] = new_max
                scores = scores - jnp.concatenate([new_max] * (2 * tok // HD), 1)
                acc_ref[rows, :] = acc_ref[rows, :] * jnp.concatenate([carry, carry], 1)
            probs = jnp.exp2(scores).astype(jnp.bfloat16)
            acc_ref[rows, :] += jnp.dot(probs, values, preferred_element_type=jnp.float32)

    def one_pair(pair, _):
        step = 2 * pair
        seen, whole = jnp.bool_(False), jnp.bool_(True)
        for i in range(2):
            src = src_ref[step + i]
            seen = seen | ((src >= 0) & (src * tok + tok - 1 >= low) & (src <= my))
            whole = whole & (src >= 0) & (src * tok >= high) & (src < my)

        @pl.when(seen & small & whole)
        def _():
            attend_pair(step, False, False)

        @pl.when(seen & small & jnp.logical_not(whole))
        def _():
            attend_pair(step, True, False)

        @pl.when(seen & jnp.logical_not(small))
        def _():
            attend_pair(step, True, True)

        return 0

    lax.fori_loop(0, (blocks + 1) // 2, one_pair, 0)
    if final:
        for h in range(GROUPS):
            acc = acc_ref[pl.ds(h * tok, tok), :]
            out_ref[:, h * HD : (h + 1) * HD] = (acc[:, :HD] / acc[:, HD:]).astype(jnp.bfloat16)


def attend(common, pieces, plan, state=None, final=False):
    query = common[-1]
    tok = query.shape[0]
    counts = tuple(piece.shape[0] // tok for piece in pieces)
    blocks = sum(counts)
    assert blocks == len(plan)
    even = blocks + blocks % 2
    vmem, smem = pl.BlockSpec(memory_space=pltpu.VMEM), pl.BlockSpec(memory_space=pltpu.SMEM)
    out_shape = (
        jax.ShapeDtypeStruct((GROUPS * tok, 2 * HD), jnp.float32),
        jax.ShapeDtypeStruct((GROUPS * tok + 8, HD), jnp.float32),
    )
    if final:
        out_shape += (jax.ShapeDtypeStruct((tok, GROUPS * HD), jnp.bfloat16),)
    flops = blocks * GROUPS * tok * tok * HD * 4
    return pl.pallas_call(
        functools.partial(attend_kernel, counts, plan, state is None, final),
        out_shape=out_shape,
        in_specs=[smem] * 5
        + [vmem] * (2 + len(pieces))
        + [vmem] * (0 if state is None else 2),
        out_specs=(vmem,) * len(out_shape),
        scratch_shapes=[
            pltpu.VMEM((tok, 2 * tok), jnp.float32),
            pltpu.VMEM((even * tok, 2 * HD), jnp.bfloat16),
            pltpu.SMEM((even,), jnp.int32),
        ],
        input_output_aliases={} if state is None else {7 + len(pieces): 0, 8 + len(pieces): 1},
        compiler_params=pltpu.CompilerParams(vmem_limit_bytes=40 << 20),
        cost_estimate=pl.CostEstimate(flops=10 * flops, bytes_accessed=4 << 20, transcendentals=0),
    )(*common, *pieces, *(state or ()))


def local(query, keys_values, doc_start, scale_index, scale_table, out_weight):
    tok = query.shape[0]
    ctx_count = lax.axis_size("ctx")
    my = lax.axis_index("ctx").astype(jnp.int32)
    starts = jnp.broadcast_to(doc_start[:, None], (tok, HD))
    squares = jnp.square(query.astype(jnp.float32)).reshape(tok, GROUPS, HD)
    norm = jnp.max(jnp.sum(squares, axis=2))
    common = (my[None], doc_start, scale_index, scale_table.T, norm[None], starts, query)

    def shifted(block, distance):
        return lax.ppermute(block, "ctx", [(i, i + distance) for i in range(ctx_count - distance)])

    def swapped(block):
        return lax.ppermute(block, "ctx", [(i, i ^ 1) for i in range(ctx_count)])

    def crossed(block):
        return lax.ppermute(block, "ctx", [(i, i ^ 2) for i in range(ctx_count)])

    def after(block, *others):
        return lax.optimization_barrier((block, *others))[0]

    def own(*back):
        return tuple((True, k, False) for k in back)

    def others(plan):
        return tuple((False, k, cross) for _, k, cross in plan)

    from_2 = shifted(keys_values, 4)
    from_02 = jnp.concatenate([keys_values, after(from_2, norm, starts)])
    from_46 = shifted(from_02, 8)
    cross_02 = crossed(from_02)
    last = [(i, i + 2) for i in range(ctx_count - 2) if i & 2]
    plan_02, plan_46, plan_8 = own(0, 2), own(4, 6), own(8)
    cplan_02, cplan_46, cplan_7 = [tuple((True, k, True) for k in ks) for ks in ((-1, 1), (3, 5), (7,))]

    swap_02 = swapped(jnp.concatenate([from_02, cross_02]))
    state = attend(common, [from_02, cross_02], plan_02 + cplan_02)
    state = attend(common, [swap_02], others(plan_02 + cplan_02), state)
    from_46 = after(from_46, *state)
    from_6 = from_46[tok:]
    cross_46 = crossed(from_46)
    from_8 = shifted(from_6, 4)
    from_7 = lax.ppermute(from_6, "ctx", last)
    state = attend(common, [from_46], plan_46, state)
    swap_46 = swapped(jnp.concatenate([from_46, from_8, from_7, after(cross_46, *state)]))
    state = attend(common, [cross_46, from_8, from_7], cplan_46 + plan_8 + cplan_7, state)
    plan = others(plan_46 + plan_8 + cplan_7 + cplan_46)
    _, _, attn = attend(common, [swap_46], plan, state, True)
    shares = lax.axis_size("kvh")
    partial = jnp.dot(attn, out_weight, preferred_element_type=jnp.float32).astype(jnp.bfloat16)
    pieces = lax.all_to_all(partial.reshape(shares, tok // shares, -1), "kvh", 0, 0)
    return jnp.sum(pieces.astype(jnp.float32), axis=0).astype(jnp.bfloat16)


def solution(mesh):
    placed = (P("ctx", "kvh"), P("ctx", "kvh"), P("ctx"), P(), P(None, "kvh"), P("kvh", None))
    return jax.shard_map(
        local, mesh=mesh, in_specs=placed, out_specs=P(("ctx", "kvh"), None), check_vma=False
    )
```

```python
import functools
import math

import jax
import jax.numpy as jnp
from jax import lax
from jax.experimental import pallas as pl
from jax.experimental.pallas import tpu as pltpu
from jax.sharding import PartitionSpec as P

H = 32
KVH = 8
HD = 128
SBLK = 128
GROUPS = H // KVH
NEG = -1e30
FACTOR = math.log2(math.e) / math.sqrt(HD)
SAFE = 80.0


def attend_kernel(
    counts, plan, first, final, my_ref, doc_ref, index_ref, table_ref, norm_ref, starts_ref, query_ref, *rest
):
    pieces, rest = rest[: len(counts)], rest[len(counts) :]
    if not first:
        rest = rest[2:]
    acc_ref, max_ref, *rest = rest
    if final:
        out_ref, *rest = rest
    bias_ref, held, src_ref = rest
    tok = query_ref.shape[0]
    parts = tok // SBLK
    flag_row = GROUPS * tok
    blocks = len(plan)
    at = 0
    for piece, count in zip(pieces, counts):
        held[pl.ds(at * tok, count * tok), :] = piece[...]
        at += count
    my, low, high = my_ref[0], doc_ref[0], doc_ref[tok - 1]
    for step, (mine, back, crossed) in enumerate(plan):
        src = (my if mine else my ^ 1) - 2 * back
        if crossed:
            src = src - 2 * (my & 2)
        src_ref[step] = src
    if blocks % 2:
        src_ref[blocks] = -1
        held[pl.ds(blocks * tok, tok), :] = jnp.zeros((tok, 2 * HD), held.dtype)
    if first:
        acc_ref[...] = jnp.zeros_like(acc_ref)

    def scale_row(step, t):
        return index_ref[jnp.clip(src_ref[step], 0, my) * parts + t]

    ones = jnp.ones((HD, HD), jnp.bfloat16)

    most = jnp.zeros((SBLK, HD), jnp.float32)
    for step in range(blocks):
        key = held[pl.ds(step * tok, tok), :HD]
        squares = jnp.dot(key * key, ones, preferred_element_type=jnp.float32)
        for t in range(parts):
            scale = table_ref[0, scale_row(step, t)] * FACTOR
            most = jnp.maximum(most, squares[t * SBLK : (t + 1) * SBLK] * (scale * scale))
    small = jnp.max(most) * norm_ref[0] <= SAFE * SAFE
    if first:
        max_ref[...] = jnp.full(max_ref.shape, jnp.where(small, 0.0, NEG), jnp.float32)
    else:
        small = small & (max_ref[flag_row, 0] > 0.0)
    max_ref[pl.ds(flag_row, 8), :] = jnp.full((8, HD), jnp.where(small, 1.0, 0.0), jnp.float32)

    def attend_pair(step, masked, shifted):
        key_scales, value_scales = [], []
        for t in range(2 * parts):
            row = scale_row(step + t // parts, t % parts)
            key_scales.append(jnp.full((1, SBLK), table_ref[0, row] * FACTOR, jnp.float32))
            value_scales.append(jnp.full((SBLK, HD), table_ref[1, row], jnp.float32))
        scale = jnp.concatenate(key_scales, 1)
        kv_rows = pl.ds(pl.multiple_of(step * tok, tok), 2 * tok)
        keys = held[kv_rows, :HD]
        values = held[kv_rows, HD:].astype(jnp.float32) * jnp.concatenate(value_scales, 0)
        values = jnp.concatenate([values.astype(jnp.bfloat16), jnp.ones((2 * tok, HD), jnp.bfloat16)], 1)
        if masked:
            column = lax.broadcasted_iota(jnp.int32, (tok, tok), 1)
            last = my * tok + lax.broadcasted_iota(jnp.int32, (tok, tok), 0)
            starts = jnp.concatenate([starts_ref[...]] * (tok // HD), 1)
            for i in range(2):
                key_pos = src_ref[step + i] * tok + column
                seen = (key_pos >= starts) & (key_pos <= last)
                bias_ref[:, i * tok : (i + 1) * tok] = jnp.where(seen, 0.0, NEG)
        for h in range(GROUPS):
            rows = pl.ds(h * tok, tok)
            scores = lax.dot_general(
                query_ref[:, h * HD : (h + 1) * HD],
                keys,
                (((1,), (1,)), ((), ())),
                preferred_element_type=jnp.float32,
            )
            scores = scores * scale
            if masked:
                scores = scores + bias_ref[...]
            if shifted:
                old_max = max_ref[rows, :]
                new_max = jnp.maximum(old_max, jnp.max(scores, axis=1, keepdims=True))
                carry = jnp.exp2(old_max - new_max)
                max_ref[rows, :] = new_max
                scores = scores - jnp.concatenate([new_max] * (2 * tok // HD), 1)
                acc_ref[rows, :] = acc_ref[rows, :] * jnp.concatenate([carry, carry], 1)
            probs = jnp.exp2(scores).astype(jnp.bfloat16)
            acc_ref[rows, :] += jnp.dot(probs, values, preferred_element_type=jnp.float32)

    def one_pair(pair, _):
        step = 2 * pair
        seen, whole = jnp.bool_(False), jnp.bool_(True)
        for i in range(2):
            src = src_ref[step + i]
            seen = seen | ((src >= 0) & (src * tok + tok - 1 >= low) & (src <= my))
            whole = whole & (src >= 0) & (src * tok >= high) & (src < my)

        @pl.when(seen & small & whole)
        def _():
            attend_pair(step, False, False)

        @pl.when(seen & small & jnp.logical_not(whole))
        def _():
            attend_pair(step, True, False)

        @pl.when(seen & jnp.logical_not(small))
        def _():
            attend_pair(step, True, True)

        return 0

    lax.fori_loop(0, (blocks + 1) // 2, one_pair, 0)
    if final:
        for h in range(GROUPS):
            acc = acc_ref[pl.ds(h * tok, tok), :]
            out_ref[:, h * HD : (h + 1) * HD] = (acc[:, :HD] / acc[:, HD:]).astype(jnp.bfloat16)


def attend(common, pieces, plan, state=None, final=False):
    query = common[-1]
    tok = query.shape[0]
    counts = tuple(piece.shape[0] // tok for piece in pieces)
    blocks = sum(counts)
    assert blocks == len(plan)
    even = blocks + blocks % 2
    vmem, smem = pl.BlockSpec(memory_space=pltpu.VMEM), pl.BlockSpec(memory_space=pltpu.SMEM)
    out_shape = (
        jax.ShapeDtypeStruct((GROUPS * tok, 2 * HD), jnp.float32),
        jax.ShapeDtypeStruct((GROUPS * tok + 8, HD), jnp.float32),
    )
    if final:
        out_shape += (jax.ShapeDtypeStruct((tok, GROUPS * HD), jnp.bfloat16),)
    flops = blocks * GROUPS * tok * tok * HD * 4
    return pl.pallas_call(
        functools.partial(attend_kernel, counts, plan, state is None, final),
        out_shape=out_shape,
        in_specs=[smem] * 5
        + [vmem] * (2 + len(pieces))
        + [vmem] * (0 if state is None else 2),
        out_specs=(vmem,) * len(out_shape),
        scratch_shapes=[
            pltpu.VMEM((tok, 2 * tok), jnp.float32),
            pltpu.VMEM((even * tok, 2 * HD), jnp.bfloat16),
            pltpu.SMEM((even,), jnp.int32),
        ],
        input_output_aliases={} if state is None else {7 + len(pieces): 0, 8 + len(pieces): 1},
        compiler_params=pltpu.CompilerParams(vmem_limit_bytes=40 << 20),
        cost_estimate=pl.CostEstimate(flops=10 * flops, bytes_accessed=4 << 20, transcendentals=0),
    )(*common, *pieces, *(state or ()))


def local(query, keys_values, doc_start, scale_index, scale_table, out_weight):
    tok = query.shape[0]
    ctx_count = lax.axis_size("ctx")
    my = lax.axis_index("ctx").astype(jnp.int32)
    starts = jnp.broadcast_to(doc_start[:, None], (tok, HD))
    squares = jnp.square(query.astype(jnp.float32)).reshape(tok, GROUPS, HD)
    norm = jnp.max(jnp.sum(squares, axis=2))
    common = (my[None], doc_start, scale_index, scale_table.T, norm[None], starts, query)

    def shifted(block, distance):
        return lax.ppermute(block, "ctx", [(i, i + distance) for i in range(ctx_count - distance)])

    def swapped(block):
        return lax.ppermute(block, "ctx", [(i, i ^ 1) for i in range(ctx_count)])

    def crossed(block):
        return lax.ppermute(block, "ctx", [(i, i ^ 2) for i in range(ctx_count)])

    def after(block, *others):
        return lax.optimization_barrier((block, *others))[0]

    def own(*back):
        return tuple((True, k, False) for k in back)

    def others(plan):
        return tuple((False, k, cross) for _, k, cross in plan)

    from_2 = shifted(keys_values, 4)
    cross_0 = crossed(keys_values)
    from_4 = shifted(keys_values, 8)
    from_2 = after(from_2, norm, starts)
    from_6 = shifted(from_2, 8)
    from_24 = jnp.concatenate([from_2, from_4])
    cross_24 = crossed(from_24)
    last = [(i, i + 2) for i in range(ctx_count - 2) if i & 2]

    def cross(*back):
        return tuple((True, k, True) for k in back)

    state = attend(common, [keys_values, from_2, cross_0], own(0, 2) + cross(-1))
    from_6 = after(from_6, *state)
    swap_024 = swapped(jnp.concatenate([keys_values, from_24, after(cross_0, from_6)]))
    cross_6 = crossed(from_6)
    from_8 = shifted(from_6, 4)
    from_7 = lax.ppermute(from_6, "ctx", last)
    plan = own(4, 6) + others(own(0, 2, 4) + cross(-1))
    state = attend(common, [from_4, from_6, swap_024], plan, state)
    swap_6 = swapped(jnp.concatenate([cross_24, from_6, from_8, from_7, after(cross_6, *state)]))
    plan = cross(1, 3, 5) + own(8) + cross(7)
    state = attend(common, [cross_24, cross_6, from_8, from_7], plan, state)
    plan = others(cross(1, 3) + own(6, 8) + cross(7, 5))
    _, _, attn = attend(common, [swap_6], plan, state, True)
    shares = lax.axis_size("kvh")
    partial = jnp.dot(attn, out_weight, preferred_element_type=jnp.float32).astype(jnp.bfloat16)
    pieces = lax.all_to_all(partial.reshape(shares, tok // shares, -1), "kvh", 0, 0)
    return jnp.sum(pieces.astype(jnp.float32), axis=0).astype(jnp.bfloat16)


def solution(mesh):
    placed = (P("ctx", "kvh"), P("ctx", "kvh"), P("ctx"), P(), P(None, "kvh"), P("kvh", None))
    return jax.shard_map(
        local, mesh=mesh, in_specs=placed, out_specs=P(("ctx", "kvh"), None), check_vma=False
    )
```

```python
import functools
import math

import jax
import jax.numpy as jnp
from jax import lax
from jax.experimental import pallas as pl
from jax.experimental.pallas import tpu as pltpu
from jax.sharding import PartitionSpec as P

H = 32
KVH = 8
HD = 128
SBLK = 128
GROUPS = H // KVH
NEG = -1e30
FACTOR = math.log2(math.e) / math.sqrt(HD)
SAFE = 80.0


def attend_kernel(
    counts, plan, first, final, my_ref, doc_ref, index_ref, table_ref, norm_ref, starts_ref, query_ref, *rest
):
    pieces, rest = rest[: len(counts)], rest[len(counts) :]
    if not first:
        rest = rest[2:]
    acc_ref, max_ref, *rest = rest
    if final:
        out_ref, *rest = rest
    bias_ref, held, src_ref = rest
    tok = query_ref.shape[0]
    parts = tok // SBLK
    flag_row = GROUPS * tok
    blocks = len(plan)
    at = 0
    for piece, count in zip(pieces, counts):
        held[pl.ds(at * tok, count * tok), :] = piece[...]
        at += count
    my, low, high = my_ref[0], doc_ref[0], doc_ref[tok - 1]
    for step, (mine, back, crossed) in enumerate(plan):
        src = (my if mine else my ^ 1) - 2 * back
        if crossed:
            src = src - 2 * (my & 2)
        src_ref[step] = src
    if blocks % 2:
        src_ref[blocks] = -1
        held[pl.ds(blocks * tok, tok), :] = jnp.zeros((tok, 2 * HD), held.dtype)
    if first:
        acc_ref[...] = jnp.zeros_like(acc_ref)

    def scale_row(step, t):
        return index_ref[jnp.clip(src_ref[step], 0, my) * parts + t]

    ones = jnp.ones((HD, HD), jnp.bfloat16)

    most = jnp.zeros((SBLK, HD), jnp.float32)
    for step in range(blocks):
        key = held[pl.ds(step * tok, tok), :HD]
        squares = jnp.dot(key * key, ones, preferred_element_type=jnp.float32)
        for t in range(parts):
            scale = table_ref[0, scale_row(step, t)] * FACTOR
            most = jnp.maximum(most, squares[t * SBLK : (t + 1) * SBLK] * (scale * scale))
    small = jnp.max(most) * norm_ref[0] <= SAFE * SAFE
    if first:
        max_ref[...] = jnp.full(max_ref.shape, jnp.where(small, 0.0, NEG), jnp.float32)
    else:
        small = small & (max_ref[flag_row, 0] > 0.0)
    max_ref[pl.ds(flag_row, 8), :] = jnp.full((8, HD), jnp.where(small, 1.0, 0.0), jnp.float32)

    def attend_pair(step, masked, shifted):
        key_scales, value_scales = [], []
        for t in range(2 * parts):
            row = scale_row(step + t // parts, t % parts)
            key_scales.append(jnp.full((1, SBLK), table_ref[0, row] * FACTOR, jnp.float32))
            value_scales.append(jnp.full((SBLK, HD), table_ref[1, row], jnp.float32))
        scale = jnp.concatenate(key_scales, 1)
        kv_rows = pl.ds(pl.multiple_of(step * tok, tok), 2 * tok)
        keys = held[kv_rows, :HD]
        values = held[kv_rows, HD:].astype(jnp.float32) * jnp.concatenate(value_scales, 0)
        values = jnp.concatenate([values.astype(jnp.bfloat16), jnp.ones((2 * tok, HD), jnp.bfloat16)], 1)
        if masked:
            column = lax.broadcasted_iota(jnp.int32, (tok, tok), 1)
            last = my * tok + lax.broadcasted_iota(jnp.int32, (tok, tok), 0)
            starts = jnp.concatenate([starts_ref[...]] * (tok // HD), 1)
            for i in range(2):
                key_pos = src_ref[step + i] * tok + column
                seen = (key_pos >= starts) & (key_pos <= last)
                bias_ref[:, i * tok : (i + 1) * tok] = jnp.where(seen, 0.0, NEG)
        for h in range(GROUPS):
            rows = pl.ds(h * tok, tok)
            scores = lax.dot_general(
                query_ref[:, h * HD : (h + 1) * HD],
                keys,
                (((1,), (1,)), ((), ())),
                preferred_element_type=jnp.float32,
            )
            scores = scores * scale
            if masked:
                scores = scores + bias_ref[...]
            if shifted:
                old_max = max_ref[rows, :]
                new_max = jnp.maximum(old_max, jnp.max(scores, axis=1, keepdims=True))
                carry = jnp.exp2(old_max - new_max)
                max_ref[rows, :] = new_max
                scores = scores - jnp.concatenate([new_max] * (2 * tok // HD), 1)
                acc_ref[rows, :] = acc_ref[rows, :] * jnp.concatenate([carry, carry], 1)
            probs = jnp.exp2(scores).astype(jnp.bfloat16)
            acc_ref[rows, :] += jnp.dot(probs, values, preferred_element_type=jnp.float32)

    def one_pair(pair, _):
        step = 2 * pair
        seen, whole = jnp.bool_(False), jnp.bool_(True)
        for i in range(2):
            src = src_ref[step + i]
            seen = seen | ((src >= 0) & (src * tok + tok - 1 >= low) & (src <= my))
            whole = whole & (src >= 0) & (src * tok >= high) & (src < my)

        @pl.when(seen & small & whole)
        def _():
            attend_pair(step, False, False)

        @pl.when(seen & small & jnp.logical_not(whole))
        def _():
            attend_pair(step, True, False)

        @pl.when(seen & jnp.logical_not(small))
        def _():
            attend_pair(step, True, True)

        return 0

    lax.fori_loop(0, (blocks + 1) // 2, one_pair, 0)
    if final:
        for h in range(GROUPS):
            acc = acc_ref[pl.ds(h * tok, tok), :]
            out_ref[:, h * HD : (h + 1) * HD] = (acc[:, :HD] / acc[:, HD:]).astype(jnp.bfloat16)


def attend(common, pieces, plan, state=None, final=False):
    query = common[-1]
    tok = query.shape[0]
    counts = tuple(piece.shape[0] // tok for piece in pieces)
    blocks = sum(counts)
    assert blocks == len(plan)
    even = blocks + blocks % 2
    vmem, smem = pl.BlockSpec(memory_space=pltpu.VMEM), pl.BlockSpec(memory_space=pltpu.SMEM)
    out_shape = (
        jax.ShapeDtypeStruct((GROUPS * tok, 2 * HD), jnp.float32),
        jax.ShapeDtypeStruct((GROUPS * tok + 8, HD), jnp.float32),
    )
    if final:
        out_shape += (jax.ShapeDtypeStruct((tok, GROUPS * HD), jnp.bfloat16),)
    flops = blocks * GROUPS * tok * tok * HD * 4
    return pl.pallas_call(
        functools.partial(attend_kernel, counts, plan, state is None, final),
        out_shape=out_shape,
        in_specs=[smem] * 5
        + [vmem] * (2 + len(pieces))
        + [vmem] * (0 if state is None else 2),
        out_specs=(vmem,) * len(out_shape),
        scratch_shapes=[
            pltpu.VMEM((tok, 2 * tok), jnp.float32),
            pltpu.VMEM((even * tok, 2 * HD), jnp.bfloat16),
            pltpu.SMEM((even,), jnp.int32),
        ],
        input_output_aliases={} if state is None else {7 + len(pieces): 0, 8 + len(pieces): 1},
        compiler_params=pltpu.CompilerParams(vmem_limit_bytes=40 << 20),
        cost_estimate=pl.CostEstimate(flops=10 * flops, bytes_accessed=4 << 20, transcendentals=0),
    )(*common, *pieces, *(state or ()))


def local(query, keys_values, doc_start, scale_index, scale_table, out_weight):
    tok = query.shape[0]
    ctx_count = lax.axis_size("ctx")
    my = lax.axis_index("ctx").astype(jnp.int32)
    starts = jnp.broadcast_to(doc_start[:, None], (tok, HD))
    squares = jnp.square(query.astype(jnp.float32)).reshape(tok, GROUPS, HD)
    norm = jnp.max(jnp.sum(squares, axis=2))
    common = (my[None], doc_start, scale_index, scale_table.T, norm[None], starts, query)

    def shifted(block, distance):
        return lax.ppermute(block, "ctx", [(i, i + distance) for i in range(ctx_count - distance)])

    def swapped(block):
        return lax.ppermute(block, "ctx", [(i, i ^ 1) for i in range(ctx_count)])

    def crossed(block):
        return lax.ppermute(block, "ctx", [(i, i ^ 2) for i in range(ctx_count)])

    def after(block, *others):
        return lax.optimization_barrier((block, *others))[0]

    def own(*back):
        return tuple((True, k, False) for k in back)

    def others(plan):
        return tuple((False, k, cross) for _, k, cross in plan)

    from_2 = shifted(keys_values, 4)
    cross_0 = crossed(keys_values)
    from_4 = shifted(keys_values, 8)
    from_2 = after(from_2, norm, starts)
    from_6 = shifted(from_2, 8)
    from_24 = jnp.concatenate([from_2, from_4])
    cross_24 = crossed(from_24)
    last = [(i, i + 2) for i in range(ctx_count - 2) if i & 2]

    def cross(*back):
        return tuple((True, k, True) for k in back)

    state = attend(common, [keys_values, from_2, cross_0], own(0, 2) + cross(-1))
    from_6 = after(from_6, *state)
    cross_6 = crossed(from_6)
    from_8 = shifted(from_6, 4)
    from_7 = lax.ppermute(from_6, "ctx", last)
    first = jnp.concatenate([keys_values, from_24, cross_0, cross_24])
    first_swap = swapped(after(first, from_6))
    state = attend(common, [from_4, from_6, cross_24], own(4, 6) + cross(1, 3), state)
    state = attend(common, [first_swap], others(own(0, 2, 4) + cross(-1, 1, 3)), state)
    from_8, from_7, cross_6, *_ = lax.optimization_barrier((from_8, from_7, cross_6, *state))
    second_swap = swapped(jnp.concatenate([from_6, from_8, from_7, cross_6]))
    state = attend(common, [cross_6, from_8, from_7], cross(5) + own(8) + cross(7), state)
    plan = others(own(6, 8) + cross(7, 5))
    _, _, attn = attend(common, [second_swap], plan, state, True)
    shares = lax.axis_size("kvh")
    partial = jnp.dot(attn, out_weight, preferred_element_type=jnp.float32).astype(jnp.bfloat16)
    pieces = lax.all_to_all(partial.reshape(shares, tok // shares, -1), "kvh", 0, 0)
    return jnp.sum(pieces.astype(jnp.float32), axis=0).astype(jnp.bfloat16)


def solution(mesh):
    placed = (P("ctx", "kvh"), P("ctx", "kvh"), P("ctx"), P(), P(None, "kvh"), P("kvh", None))
    return jax.shard_map(
        local, mesh=mesh, in_specs=placed, out_specs=P(("ctx", "kvh"), None), check_vma=False
    )
```

```python
import functools
import math

import jax
import jax.numpy as jnp
from jax import lax
from jax.experimental import pallas as pl
from jax.experimental.pallas import tpu as pltpu
from jax.sharding import PartitionSpec as P

H = 32
KVH = 8
HD = 128
SBLK = 128
GROUPS = H // KVH
NEG = -1e30
FACTOR = math.log2(math.e) / math.sqrt(HD)
SAFE = 80.0


def attend_kernel(
    counts, plan, first, final, my_ref, doc_ref, index_ref, table_ref, norm_ref, starts_ref, query_ref, *rest
):
    pieces, rest = rest[: len(counts)], rest[len(counts) :]
    if not first:
        rest = rest[2:]
    acc_ref, max_ref, *rest = rest
    if final:
        out_ref, *rest = rest
    bias_ref, held, src_ref = rest
    tok = query_ref.shape[0]
    parts = tok // SBLK
    flag_row = GROUPS * tok
    blocks = len(plan)
    at = 0
    for piece, count in zip(pieces, counts):
        held[pl.ds(at * tok, count * tok), :] = piece[...]
        at += count
    my, low, high = my_ref[0], doc_ref[0], doc_ref[tok - 1]
    for step, (mine, back, crossed) in enumerate(plan):
        src = (my if mine else my ^ 1) - 2 * back
        if crossed:
            src = src - 2 * (my & 2)
        src_ref[step] = src
    if blocks % 2:
        src_ref[blocks] = -1
        held[pl.ds(blocks * tok, tok), :] = jnp.zeros((tok, 2 * HD), held.dtype)
    if first:
        acc_ref[...] = jnp.zeros_like(acc_ref)

    def scale_row(step, t):
        return index_ref[jnp.clip(src_ref[step], 0, my) * parts + t]

    ones = jnp.ones((HD, HD), jnp.bfloat16)

    most = jnp.zeros((SBLK, HD), jnp.float32)
    for step in range(blocks):
        key = held[pl.ds(step * tok, tok), :HD]
        squares = jnp.dot(key * key, ones, preferred_element_type=jnp.float32)
        for t in range(parts):
            scale = table_ref[0, scale_row(step, t)] * FACTOR
            most = jnp.maximum(most, squares[t * SBLK : (t + 1) * SBLK] * (scale * scale))
    small = jnp.max(most) * norm_ref[0] <= SAFE * SAFE
    if first:
        max_ref[...] = jnp.full(max_ref.shape, jnp.where(small, 0.0, NEG), jnp.float32)
    else:
        small = small & (max_ref[flag_row, 0] > 0.0)
    max_ref[pl.ds(flag_row, 8), :] = jnp.full((8, HD), jnp.where(small, 1.0, 0.0), jnp.float32)

    def attend_pair(step, masked, shifted):
        key_scales, value_scales = [], []
        for t in range(2 * parts):
            row = scale_row(step + t // parts, t % parts)
            key_scales.append(jnp.full((1, SBLK), table_ref[0, row] * FACTOR, jnp.float32))
            value_scales.append(jnp.full((SBLK, HD), table_ref[1, row], jnp.float32))
        scale = jnp.concatenate(key_scales, 1)
        kv_rows = pl.ds(pl.multiple_of(step * tok, tok), 2 * tok)
        keys = held[kv_rows, :HD]
        values = held[kv_rows, HD:].astype(jnp.float32) * jnp.concatenate(value_scales, 0)
        values = jnp.concatenate([values.astype(jnp.bfloat16), jnp.ones((2 * tok, HD), jnp.bfloat16)], 1)
        if masked:
            column = lax.broadcasted_iota(jnp.int32, (tok, tok), 1)
            last = my * tok + lax.broadcasted_iota(jnp.int32, (tok, tok), 0)
            starts = jnp.concatenate([starts_ref[...]] * (tok // HD), 1)
            for i in range(2):
                key_pos = src_ref[step + i] * tok + column
                seen = (key_pos >= starts) & (key_pos <= last)
                bias_ref[:, i * tok : (i + 1) * tok] = jnp.where(seen, 0.0, NEG)
        for h in range(GROUPS):
            rows = pl.ds(h * tok, tok)
            scores = lax.dot_general(
                query_ref[:, h * HD : (h + 1) * HD],
                keys,
                (((1,), (1,)), ((), ())),
                preferred_element_type=jnp.float32,
            )
            scores = scores * scale
            if masked:
                scores = scores + bias_ref[...]
            if shifted:
                old_max = max_ref[rows, :]
                new_max = jnp.maximum(old_max, jnp.max(scores, axis=1, keepdims=True))
                carry = jnp.exp2(old_max - new_max)
                max_ref[rows, :] = new_max
                scores = scores - jnp.concatenate([new_max] * (2 * tok // HD), 1)
                acc_ref[rows, :] = acc_ref[rows, :] * jnp.concatenate([carry, carry], 1)
            probs = jnp.exp2(scores).astype(jnp.bfloat16)
            acc_ref[rows, :] += jnp.dot(probs, values, preferred_element_type=jnp.float32)

    def one_pair(pair, _):
        step = 2 * pair
        seen, whole = jnp.bool_(False), jnp.bool_(True)
        for i in range(2):
            src = src_ref[step + i]
            seen = seen | ((src >= 0) & (src * tok + tok - 1 >= low) & (src <= my))
            whole = whole & (src >= 0) & (src * tok >= high) & (src < my)

        @pl.when(seen & small & whole)
        def _():
            attend_pair(step, False, False)

        @pl.when(seen & small & jnp.logical_not(whole))
        def _():
            attend_pair(step, True, False)

        @pl.when(seen & jnp.logical_not(small))
        def _():
            attend_pair(step, True, True)

        return 0

    lax.fori_loop(0, (blocks + 1) // 2, one_pair, 0)
    if final:
        for h in range(GROUPS):
            acc = acc_ref[pl.ds(h * tok, tok), :]
            out_ref[:, h * HD : (h + 1) * HD] = (acc[:, :HD] / acc[:, HD:]).astype(jnp.bfloat16)


def attend(common, pieces, plan, state=None, final=False):
    query = common[-1]
    tok = query.shape[0]
    counts = tuple(piece.shape[0] // tok for piece in pieces)
    blocks = sum(counts)
    assert blocks == len(plan)
    even = blocks + blocks % 2
    vmem, smem = pl.BlockSpec(memory_space=pltpu.VMEM), pl.BlockSpec(memory_space=pltpu.SMEM)
    out_shape = (
        jax.ShapeDtypeStruct((GROUPS * tok, 2 * HD), jnp.float32),
        jax.ShapeDtypeStruct((GROUPS * tok + 8, HD), jnp.float32),
    )
    if final:
        out_shape += (jax.ShapeDtypeStruct((tok, GROUPS * HD), jnp.bfloat16),)
    flops = blocks * GROUPS * tok * tok * HD * 4
    return pl.pallas_call(
        functools.partial(attend_kernel, counts, plan, state is None, final),
        out_shape=out_shape,
        in_specs=[smem] * 5
        + [vmem] * (2 + len(pieces))
        + [vmem] * (0 if state is None else 2),
        out_specs=(vmem,) * len(out_shape),
        scratch_shapes=[
            pltpu.VMEM((tok, 2 * tok), jnp.float32),
            pltpu.VMEM((even * tok, 2 * HD), jnp.bfloat16),
            pltpu.SMEM((even,), jnp.int32),
        ],
        input_output_aliases={} if state is None else {7 + len(pieces): 0, 8 + len(pieces): 1},
        compiler_params=pltpu.CompilerParams(vmem_limit_bytes=40 << 20),
        cost_estimate=pl.CostEstimate(flops=10 * flops, bytes_accessed=4 << 20, transcendentals=0),
    )(*common, *pieces, *(state or ()))


def local(query, keys_values, doc_start, scale_index, scale_table, out_weight):
    tok = query.shape[0]
    ctx_count = lax.axis_size("ctx")
    my = lax.axis_index("ctx").astype(jnp.int32)
    starts = jnp.broadcast_to(doc_start[:, None], (tok, HD))
    squares = jnp.square(query.astype(jnp.float32)).reshape(tok, GROUPS, HD)
    norm = jnp.max(jnp.sum(squares, axis=2))
    common = (my[None], doc_start, scale_index, scale_table.T, norm[None], starts, query)

    def shifted(block, distance):
        return lax.ppermute(block, "ctx", [(i, i + distance) for i in range(ctx_count - distance)])

    def swapped(block):
        return lax.ppermute(block, "ctx", [(i, i ^ 1) for i in range(ctx_count)])

    def crossed(block):
        return lax.ppermute(block, "ctx", [(i, i ^ 2) for i in range(ctx_count)])

    def after(block, *others):
        return lax.optimization_barrier((block, *others))[0]

    def own(*back):
        return tuple((True, k, False) for k in back)

    def others(plan):
        return tuple((False, k, cross) for _, k, cross in plan)

    from_2 = shifted(keys_values, 4)
    cross_0 = crossed(keys_values)
    from_4 = shifted(keys_values, 8)
    from_2 = after(from_2, norm, starts)
    from_6 = shifted(from_2, 8)
    from_24 = jnp.concatenate([from_2, from_4])
    cross_24 = crossed(from_24)
    last = [(i, i + 2) for i in range(ctx_count - 2) if i & 2]

    def cross(*back):
        return tuple((True, k, True) for k in back)

    state = attend(common, [keys_values, from_2, cross_0], own(0, 2) + cross(-1))
    swap_024 = swapped(jnp.concatenate([keys_values, from_24, after(cross_0, from_6)]))
    from_6 = after(from_6, *state, cross_24)
    cross_6 = crossed(from_6)
    from_8 = shifted(from_6, 4)
    from_7 = lax.ppermute(from_6, "ctx", last)
    plan = own(4, 6) + cross(1, 3) + others(own(0, 2, 4) + cross(-1))
    state = attend(common, [from_4, from_6, cross_24, swap_024], plan, state)
    from_8, from_7, cross_6, *_ = lax.optimization_barrier((from_8, from_7, cross_6, *state))
    swap_6 = swapped(jnp.concatenate([cross_24, from_6, from_8, from_7, cross_6]))
    state = attend(common, [cross_6, from_8, from_7], cross(5) + own(8) + cross(7), state)
    plan = others(cross(1, 3) + own(6, 8) + cross(7, 5))
    _, _, attn = attend(common, [swap_6], plan, state, True)
    shares = lax.axis_size("kvh")
    partial = jnp.dot(attn, out_weight, preferred_element_type=jnp.float32).astype(jnp.bfloat16)
    pieces = lax.all_to_all(partial.reshape(shares, tok // shares, -1), "kvh", 0, 0)
    return jnp.sum(pieces.astype(jnp.float32), axis=0).astype(jnp.bfloat16)


def solution(mesh):
    placed = (P("ctx", "kvh"), P("ctx", "kvh"), P("ctx"), P(), P(None, "kvh"), P("kvh", None))
    return jax.shard_map(
        local, mesh=mesh, in_specs=placed, out_specs=P(("ctx", "kvh"), None), check_vma=False
    )
```
